256 devices in a mesh: tm: 16 (over y, x), space: 16 (over z, core).
Axes of the slice: x: 4, y: 4, z: 8, core: 2. Of those that a mesh axis runs over, the one named last changes fastest.
Arguments:
- iterate: float32 [16, 16, 256, 1024], P('tm', None, 'space'), may hold values from -1.2 to 1.2
- fine_prev: float32 [16, 16, 256, 1024], P('tm', None, 'space'), may hold values from -1.2 to 1.2
- mobility: float32 [16, 256, 1024], P(None, 'space'), may hold values from 0.5 to 4
- pending: int32 [16], replicated, may hold values 0 or 1
Outputs:
- slice_ends: float32 [16, 16, 256, 1024], P('tm', None, 'space')
The draws below stay inside these ranges and needn't reach their ends.
All inputs are finite; a program needn't handle non-finite values.
Results may differ from the reference program's by a relative error of at most 0.0003.
Values sent between devices are 32-bit elements; how exact they have to be, the bound alone decides.
No kernel may reach another device: no remote copies, remote signals or barrier semaphores. Data moves between devices by JAX's collectives and lax.ppermute only.
A program may use at most 256 MiB of HBM per device.

```python
import math
import jax
import jax.numpy as jnp
from jax import lax

Z = 16
NY = 1024
FINE_STEPS = 2
NT = 16
NX = 256


def plant(array, stream_key, low, top_value):
    shape = array.shape
    index_at = [jax.random.randint(jax.random.fold_in(stream_key, axis), (), 0, shape[axis]) for axis in range(len(shape))]
    array = array.at[tuple(index_at)].set(low)
    longest = shape.index(max(shape))
    index_at[longest] = (index_at[longest] + 1) % shape[longest]
    return array.at[tuple(index_at)].set(top_value)


def block_scale(key, shape, split, low, largest):
    level, own = 1.0, jax.random.fold_in(key, 6)
    for dim, blocks in split:
        steps = jnp.exp(jax.random.uniform(jax.random.fold_in(own, dim), (blocks,), jnp.float32, low / len(split), largest / len(split)))
        level = level * jnp.repeat(steps, shape[dim] // blocks).reshape([-1 if axis == dim else 1 for axis in range(len(shape))])
    return level


def setup_inputs(seed: int = 0) -> dict:
    key_list = jax.random.split(jax.random.key(seed), 5)
    return {
        "iterate": jnp.clip(jax.random.uniform(key_list[0], (NT, Z, NX, NY), jnp.float32, -1.2, 1.2) * block_scale(key_list[0], (NT, Z, NX, NY), ((0, 16), (2, 16)), -0.4, 0.0), -1.2, 1.2),
        "fine_prev": jnp.clip(jax.random.uniform(key_list[1], (NT, Z, NX, NY), jnp.float32, -1.2, 1.2) * block_scale(key_list[1], (NT, Z, NX, NY), ((0, 16), (2, 16)), -0.4, 0.0), -1.2, 1.2),
        "mobility": jnp.clip(jnp.exp(math.log(4.0) - 2.0794415 * jax.random.uniform(key_list[2], (Z, NX, NY), jnp.float32) ** block_scale(key_list[2], (Z, NX, NY), ((1, 16),), -0.2, 0.2)), 0.5, 4.0),
        "pending": plant((jax.random.randint(key_list[3], (NT,), 0, 2) < 1).astype(jnp.int32), jax.random.fold_in(key_list[3], 1), 0, 1),
    }


DIFFUSE = 0.15
REACTION = 0.1


def update(padded, mobility_rows):
    center = padded[:, 1:-1, :]
    framed = jnp.pad(padded, ((1, 1), (0, 0), (1, 1)))
    laplace = (framed[2:, 1:-1, 1:-1] + framed[:-2, 1:-1, 1:-1]) + (framed[1:-1, 2:, 1:-1] + framed[1:-1, :-2, 1:-1]) + (framed[1:-1, 1:-1, 2:] + framed[1:-1, 1:-1, :-2]) - 6.0 * center
    return center + DIFFUSE * laplace + REACTION * mobility_rows * (center - center * center * center)


def coarse_update(padded, coarse_mobility):
    center = padded[:, 1:-1, :]
    framed = jnp.pad(padded, ((1, 1), (0, 0), (1, 1)))
    along_x = framed[1:-1, 2:, 1:-1] + framed[1:-1, :-2, 1:-1] - 2.0 * center
    along_y = framed[1:-1, 1:-1, 2:] + framed[1:-1, 1:-1, :-2] - 2.0 * center
    along_z = framed[2:, 1:-1, 1:-1] + framed[:-2, 1:-1, 1:-1] - 2.0 * center
    laplace = 0.25 * along_x + 0.25 * along_y + along_z
    rate = 2.0 * REACTION * coarse_mobility
    return center + 2.0 * DIFFUSE * laplace + rate * (center - center * center * center) / (1.0 + rate * center * center)


def restrict(field):
    layer_count, row_count, col_count = field.shape
    blocks = field.reshape(layer_count, row_count // 2, 2, col_count // 2, 2)
    return 0.25 * jnp.sum(blocks, axis=(2, 4))


def pad_rows(field):
    return jnp.pad(field, ((0, 0), (1, 1), (0, 0)))


def reference(iterate, fine_prev, mobility, pending):
    coarse_mobility = restrict(mobility)

    def per_slice(slice_items):
        start_state, previous, flagged = slice_items
        fine_state = start_state
        for _ in range(FINE_STEPS):
            fine_state = update(pad_rows(fine_state), mobility)
        fine_state = jnp.where(flagged > 0, fine_state, previous)
        coarse_old = coarse_update(pad_rows(restrict(start_state)), coarse_mobility)
        return fine_state, coarse_old, restrict(fine_state) - coarse_old

    fines, coarse_olds, jump_terms = lax.map(per_slice, (iterate, fine_prev, pending))

    def advance_link(coarse_now, jump_now):
        advanced = coarse_update(pad_rows(coarse_now), coarse_mobility)
        return advanced + jump_now, advanced

    _, advanced_all = lax.scan(advance_link, restrict(iterate[0]), jump_terms)
    correction = advanced_all - coarse_olds
    return fines + jnp.repeat(jnp.repeat(correction, 2, axis=2), 2, axis=3)
```

```python
import jax
import jax.numpy as jnp
from jax import lax
from jax.experimental import pallas as pl
from jax.experimental.pallas import tpu as pltpu
from jax.sharding import PartitionSpec as P

Z = 16
X = 16
Y = 1024
T = 16
S = 16
CX = X // 2
CY = Y // 2
ROWS = Z * X
CROWS = Z * CX
OWN = CY // T
MARGIN = 16
HALF = Z // 2
FIRST = 7
SPAN = 3 * CX

DIFFUSE = 0.15
REACTION = 0.1
VMEM_LIMIT = 48 * 1024 * 1024
PACK_VMEM = 54272 * 1024


MOBILITY = T
EARLY = (
    ((0, 7), (6, 1)),
    ((1, 6), (5, 2)),
    ((2, 5), (4, 3)),
    ((3, 4), (MOBILITY, 4)),
)
LATE = (
    ((8, 7), (14, 1)),
    ((9, 6), (13, 2)),
    ((10, 5), (12, 3)),
)
LAST = 11
EARLY_TILES = len(EARLY) * HALF + 2
LATE_TILES = (len(LATE) + 1) * HALF


def call(body, outs, scratch=(), flops=0):
    return pl.pallas_call(
        body,
        out_shape=[jax.ShapeDtypeStruct(shape, jnp.float32) for shape in outs],
        scratch_shapes=[pltpu.VMEM(shape, jnp.float32) for shape in scratch],
        compiler_params=pltpu.CompilerParams(vmem_limit_bytes=VMEM_LIMIT),
        cost_estimate=pl.CostEstimate(flops=flops, bytes_accessed=4_000_000, transcendentals=0),
    )


def iota(shape, axis):
    return lax.broadcasted_iota(jnp.int32, shape, axis)


def split(value):
    high = value.astype(jnp.bfloat16)
    low = (value - high.astype(jnp.float32)).astype(jnp.bfloat16)
    return high, low


def restrict(value, parts):
    high, low = split(value)
    pick = (iota((256, 128), 0) // 2 == iota((256, 128), 1)).astype(jnp.bfloat16)
    for k in range(Y // 256):
        chunk = slice(256 * k, 256 * (k + 1))
        parts[k] = jnp.dot(high[:, chunk], pick, preferred_element_type=jnp.float32) + jnp.dot(
            low[:, chunk], pick, preferred_element_type=jnp.float32
        )
    pieces = [
        parts[k, pl.ds(0, CROWS, stride=2), :] + parts[k, pl.ds(1, CROWS, stride=2), :]
        for k in range(Y // 256)
    ]
    return 0.25 * jnp.concatenate(pieces, axis=1)


def halve_lanes(value):
    high, low = split(value)
    pick = (iota((256, 128), 0) // 2 == iota((256, 128), 1)).astype(jnp.bfloat16)
    pieces = []
    for k in range(Y // 256):
        chunk = slice(256 * k, 256 * (k + 1))
        pieces.append(
            jnp.dot(high[:, chunk], pick, preferred_element_type=jnp.float32)
            + jnp.dot(low[:, chunk], pick, preferred_element_type=jnp.float32)
        )
    return jnp.concatenate(pieces, axis=1)


def beside_lanes(value):
    count = value.shape[-1]
    axis = value.ndim - 1
    before = pltpu.roll(value, 1, axis)
    after = pltpu.roll(value, count - 1, axis)
    lane = iota(value.shape[:-1] + (128,), axis)
    before = jnp.concatenate(
        [jnp.where(lane == 0, 0.0, before[..., :128]), before[..., 128:]], axis=axis
    )
    after = jnp.concatenate(
        [after[..., :-128], jnp.where(lane == 127, 0.0, after[..., -128:])], axis=axis
    )
    return before + after


def fine_rule(center, around, mobility):
    return DIFFUSE * around + REACTION * (center * (1.0 + mobility * (1.0 - center * center)))


def fine_tile(ref, mob_ref, z, tile, low_row, high_row):
    base = z * X + tile * 8
    center = ref[pl.ds(base, 8), :]
    row = iota((8, Y), 0)
    below = ref[pl.ds(base - 1, 1), :] if tile else low_row
    above = high_row if tile else ref[pl.ds(base + 8, 1), :]
    around = jnp.where(row == 0, below, pltpu.roll(center, 1, 0))
    around += jnp.where(row == 7, above, pltpu.roll(center, 7, 0))
    around += beside_lanes(center)
    if z > 0:
        around += ref[pl.ds(base - X, 8), :]
    if z < Z - 1:
        around += ref[pl.ds(base + X, 8), :]
    return fine_rule(center, around, mob_ref[pl.ds(base, 8), :])


def pack_fine_body(iterate, mobility, odd, even, done):
    space = lax.axis_index("space")

    def put(low, high):
        moves = []
        for out, near, far in ((low, 0, 1), (high, X - 1, X - 2)):
            for k, (source, inner) in enumerate(((iterate, near), (iterate, far), (mobility, near))):
                moves.append(
                    pltpu.make_async_copy(source.at[:, inner, :], out.at[k], done.at[len(moves)])
                )
        for move in moves:
            move.start()
        for move in moves:
            move.wait()

    pl.when(space % 2 == 0)(lambda: put(odd, even))
    pl.when(space % 2 == 1)(lambda: put(even, odd))


def windows(value):
    count = CY // 128
    blank = jnp.zeros((HALF, CX, 128), jnp.float32)
    lane = iota((HALF, CX, 128), 2)
    moved = {}

    def piece(half, index, amount):
        if not 0 <= index < count:
            return blank
        if (half, index, amount) not in moved:
            planes = value[HALF * half : HALF * (half + 1)]
            moved[half, index, amount] = pltpu.roll(
                planes[:, :, 128 * index : 128 * (index + 1)], amount, 2
            )
        return moved[half, index, amount]

    tiles = []
    for tile in range(T):
        start = tile * OWN - MARGIN
        first = start // 128
        offset = start - first * 128
        parts = []
        for half in range(2):
            amount = (64 * half - offset) % 128
            part = piece(half, first, amount)
            if offset + 64 > 128:
                after = piece(half, first + 1, amount)
                part = jnp.where(lane < 64 * half + 128 - offset, part, after)
            parts.append(part)
        tiles.append(jnp.where(lane < 64, parts[0], parts[1]))
    return tiles


def turned(value, tile):
    start = tile * OWN - MARGIN
    wide = jnp.concatenate([value, jnp.zeros((Z, CX, 128), jnp.float32)], axis=2)
    count = CY + 128
    first = pltpu.roll(wide[:HALF], (count - start) % count, 2)[:, :, :128]
    second = pltpu.roll(wide[HALF:], (count - start + 64) % count, 2)[:, :, :128]
    return jnp.where(iota((HALF, CX, 128), 2) < 64, first, second)


def partial_step(source, mobility, target):
    none = jnp.zeros((1, Y), jnp.float32)
    for z in range(Z):
        for tile in range(X // 8):
            target[pl.ds(z * X + tile * 8, 8), :] = fine_tile(
                source, mobility, z, tile, none, none
            )


def before_body(pending, iterate, mobility, stepped, coarse_old, mob_tile, outer, flag, parts):
    turn = lax.axis_index("tm")
    mine = jnp.where(iota((1, T), 1) == turn, pending[...], 0)
    chosen = jnp.sum(mine, axis=1, keepdims=True)
    flag[...] = jnp.broadcast_to(jnp.where(chosen > 0, 1.0, 0.0), (8, 128))
    partial_step(iterate, mobility, stepped)
    for side, inner in ((0, 0), (1, X - 1)):
        for z in range(Z):
            outer[side, pl.ds(z, 1), :] = stepped[pl.ds(z * X + inner, 1), :]
    coarse_mobility = restrict(mobility[...], parts).reshape(Z, CX, CY)
    start = restrict(iterate[...], parts).reshape(Z, CX, CY)
    row = iota((Z, CX, CY), 1)
    around = jnp.where(row == 0, 0.0, pltpu.roll(start, 1, 1))
    around += jnp.where(row == CX - 1, 0.0, pltpu.roll(start, CX - 1, 1))
    around += beside_lanes(start)
    flat = jnp.zeros((1, CX, CY), jnp.float32)
    stacked = jnp.concatenate([start[1:], flat], axis=0)
    stacked += jnp.concatenate([flat, start[:-1]], axis=0)
    rate = 2.0 * REACTION * coarse_mobility
    kept, given = coarse_rule(start, 0.5 * DIFFUSE * around, stacked, rate)
    coarse_old[...] = (kept + given).reshape(CROWS, CY)
    mob_tile[...] = turned(coarse_mobility, turn)


def second_body(flag, stepped, mobility, coarse_old, previous, fine, sent, parts):
    turn = lax.axis_index("tm")
    flagged = jnp.max(flag[...]) > 0.5
    pl.when(flagged)(lambda: partial_step(stepped, mobility, fine))

    @pl.when(jnp.logical_not(flagged))
    def _():
        fine[...] = previous[...]

    weight = jnp.where(turn > 0, 1.0, 0.0)
    term = restrict(fine[...], parts) - weight * coarse_old[...]
    for tile, value in enumerate(windows(term.reshape(Z, CX, CY))):
        sent[tile] = value


def coarse_rule(center, beside, stacked, rate):
    bottom = 1.0 + rate * (center * center)
    inverse = pltpu.reciprocal(bottom, approx=True)
    inverse = inverse * (2.0 - bottom * inverse)
    kept = center * ((1.0 + rate) * inverse - 6.0 * DIFFUSE)
    return kept, beside + 2.0 * DIFFUSE * stacked


def edge_windows(value):
    count = CY // 128
    lane = iota((HALF, 128), 1)
    moved = {}

    def piece(half, index, amount):
        if not 0 <= index < count:
            return jnp.zeros((HALF, 128), jnp.float32)
        if (half, index, amount) not in moved:
            part = value[HALF * half : HALF * (half + 1), 128 * index : 128 * (index + 1)]
            moved[half, index, amount] = pltpu.roll(part, amount, 1)
        return moved[half, index, amount]

    tiles = []
    for tile in range(T):
        start = tile * OWN - MARGIN
        first = start // 128
        offset = start - first * 128
        parts = []
        for half in range(2):
            amount = (64 * half - offset) % 128
            part = piece(half, first, amount)
            if offset + 64 > 128:
                after = piece(half, first + 1, amount)
                part = jnp.where(lane < 64 * half + 128 - offset, part, after)
            parts.append(part)
        tiles.append(jnp.where(lane < 64, parts[0], parts[1]))
    return tiles


def edge_body(
    flag, own_odd, own_even, odd, even, outer, sent_in, sent, change, old_change, halo, added_rows
):
    space = lax.axis_index("space")
    turn = lax.axis_index("tm")

    def take(low, high, own_low, own_high):
        for side, (got, own) in enumerate(((low, own_low), (high, own_high))):
            for k in range(3):
                halo[side, k] = got[k]
            halo[side, 3] = own[0]
            halo[side, 4] = own[2]

    pl.when(space % 2 == 0)(lambda: take(odd, even, own_odd, own_even))
    pl.when(space % 2 == 1)(lambda: take(even, odd, own_even, own_odd))

    flagged = flag[pl.ds(0, 1), pl.ds(0, 1)]
    weight = jnp.where(turn > 0, 1.0, 0.0)
    plane = iota((Z, Y), 0)

    def beside(value):
        total = jnp.where(plane == 0, 0.0, pltpu.roll(value, 1, 0))
        total += jnp.where(plane == Z - 1, 0.0, pltpu.roll(value, Z - 1, 0))
        return total + beside_lanes(value)

    sums = [None] * 4
    for side, inside in ((0, space > 0), (1, space < S - 1)):
        keep = jnp.where(inside, 1.0, 0.0)
        near, far, mob = keep * halo[side, 0], keep * halo[side, 1], halo[side, 2]
        own, own_mob = halo[side, 3], halo[side, 4]
        beyond = keep * fine_rule(near, far + own + beside(near), mob)
        added = DIFFUSE * near
        before = outer[side]
        after = before + added
        grown = after * (1.0 - after * after) - before * (1.0 - before * before)
        first = added + DIFFUSE * (beyond + beside(added) - 6.0 * added)
        first = flagged * (first + REACTION * own_mob * grown)
        second = flagged * DIFFUSE * added
        change[side, 0] = first
        change[side, 1] = second
        sums[side] = near + far
        sums[2 + side] = first + second
    halved = halve_lanes(jnp.concatenate(sums, axis=0))
    for side in range(2):
        coarse_side = (0.5 * DIFFUSE * 0.25) * halved[side * Z : (side + 1) * Z]
        fine_side = 0.25 * halved[(2 + side) * Z : (3 + side) * Z]
        old_change[side] = coarse_side
        for tile, value in enumerate(edge_windows(fine_side - weight * coarse_side)):
            added_rows[side, tile] = value
    row = iota((CX, 128), 0)
    for tile in range(T):
        for z in range(HALF):
            low = added_rows[0, tile, pl.ds(z, 1), :]
            high = added_rows[1, tile, pl.ds(z, 1), :]
            change_here = jnp.where(row == 0, low, jnp.where(row == CX - 1, high, 0.0))
            sent[tile, z] = sent_in[tile, z] + change_here


def repair_body(fine_in, change, old_in, old_change, fine, coarse_old):
    row = iota((8, Y), 0)
    coarse_row = iota((CX, CY), 0)
    for z in range(Z):
        for side in range(2):
            here = pl.ds(z * X + side * 8, 8)
            first = change[side, 0, pl.ds(z, 1), :]
            second = change[side, 1, pl.ds(z, 1), :]
            last = 7 * side
            added = jnp.where(row == last, first, jnp.where(row == abs(last - 1), second, 0.0))
            fine[here, :] = fine_in[here, :] + added
        here = pl.ds(z * CX, CX)
        low, high = old_change[0, pl.ds(z, 1), :], old_change[1, pl.ds(z, 1), :]
        added = jnp.where(coarse_row == 0, low, jnp.where(coarse_row == CX - 1, high, 0.0))
        coarse_old[here, :] = old_in[here, :] + added


def pack_chain_body(terms, mob_tile, odd, even, late_odd, late_even):
    space = lax.axis_index("space")
    row = iota((HALF, CX, 128), 1)

    def of(number):
        return mob_tile[...] if number == MOBILITY else terms[number]

    def put(low, high, late_low, late_high):
        for pairs, first, last in ((EARLY, low, high), (LATE, late_low, late_high)):
            for k, ((one, rows), (other, rest)) in enumerate(pairs):
                here, there = of(one), of(other)
                place = pl.ds(k * HALF, HALF)
                first[place] = jnp.where(row < rows, here, pltpu.roll(there, rows, 1))
                last[place] = jnp.where(row >= rest, here, pltpu.roll(there, rest, 1))
        for k in range(2):
            for z in range(HALF):
                low[EARLY_TILES - 2 + k, pl.ds(z, 1), :] = mob_tile[z, pl.ds(4 + k, 1), :]
                high[EARLY_TILES - 2 + k, pl.ds(z, 1), :] = mob_tile[z, pl.ds(2 + k, 1), :]
        place = pl.ds(len(LATE) * HALF, HALF)
        late_low[place] = jnp.where(row < 4, terms[LAST], mob_tile[...])
        late_high[place] = jnp.where(row >= 4, terms[LAST], mob_tile[...])

    pl.when(space % 2 == 0)(lambda: put(odd, even, late_odd, late_even))
    pl.when(space % 2 == 1)(lambda: put(even, odd, late_even, late_odd))


def chain_parts(terms, shipments):
    place = {}
    for pairs, low, high in shipments:
        for k, ((one, rows), (other, rest)) in enumerate(pairs):
            place[one] = (low, high, k, 0, 0)
            place[other] = (low, high, k, CX - rest, CX - rows)

    def extended(number):
        own = terms[number]
        if number not in place:
            return jnp.concatenate([jnp.zeros_like(own), own, jnp.zeros_like(own)], axis=1)
        low, high, k, up, down = place[number]
        below, above = low[pl.ds(k * HALF, HALF)], high[pl.ds(k * HALF, HALF)]
        if up:
            below = pltpu.roll(below, up, 1)
            above = pltpu.roll(above, down, 1)
        return jnp.concatenate([below, own, above], axis=1)

    return extended


def inner_mobility(low, high):
    place = pl.ds((len(EARLY) - 1) * HALF, HALF)
    return pltpu.roll(low[place], 4, 1), pltpu.roll(high[place], 4, 1)


def early_mobility(low, high):
    below, above = inner_mobility(low, high)
    row = iota((CX, 128), 0)
    lows, highs = [], []
    for z in range(HALF):
        low_rows = [low[EARLY_TILES - 2 + k, pl.ds(z, 1), :] for k in range(2)]
        high_rows = [high[EARLY_TILES - 2 + k, pl.ds(z, 1), :] for k in range(2)]
        outer = jnp.where(row == 2, low_rows[0], jnp.where(row == 3, low_rows[1], 0.0))
        lows.append(jnp.where(row >= 4, below[z], outer)[None])
        outer = jnp.where(row == 4, high_rows[0], jnp.where(row == 5, high_rows[1], 0.0))
        highs.append(jnp.where(row < 4, above[z], outer)[None])
    return jnp.concatenate(lows, axis=0), jnp.concatenate(highs, axis=0)


def late_mobility(low, high, late_low, late_high):
    below, above = inner_mobility(low, high)
    place = pl.ds(len(LATE) * HALF, HALF)
    row = iota((HALF, CX, 128), 1)
    return (
        jnp.where(row >= 4, below, late_low[place]),
        jnp.where(row < 4, above, late_high[place]),
    )


def around_chain(space, turn):
    row = iota((1, SPAN, 128), 1) - CX + space * CX
    column = iota((1, SPAN, 128), 2) % 64 - MARGIN + turn * OWN
    inside = (row >= 0) & (row < S * CX) & (column >= 0) & (column < CY)
    return jnp.where(inside, 0.5 * DIFFUSE, 0.0)


def chain_step(state, rate, weight):
    lane = iota((1, SPAN, 128), 2)
    crossed_up = jnp.where(lane < 64, pltpu.roll(state[:1], 64, 2), 0.0)
    crossed_down = jnp.where(lane >= 64, pltpu.roll(state[HALF - 1 :], 64, 2), 0.0)
    stacked = jnp.concatenate([state[1:], crossed_up], axis=0)
    stacked += jnp.concatenate([crossed_down, state[:-1]], axis=0)
    beside = pltpu.roll(state, 1, 1) + pltpu.roll(state, SPAN - 1, 1)
    beside += pltpu.roll(state, 1, 2) + pltpu.roll(state, 127, 2)
    return coarse_rule(state, weight * beside, stacked, rate)


def returned(advanced):
    own = advanced[:, CX : 2 * CX, :]
    lane = iota((4, CX, 128), 2)
    return jnp.where(
        lane % 64 < OWN,
        pltpu.roll(own[:4], 128 - MARGIN, 2),
        pltpu.roll(own[4:], OWN - MARGIN, 2),
    )


def run_chain(state, extended, rate, weight, numbers, back):
    for number in numbers:
        kept, given = chain_step(state, rate, weight)
        back[number] = returned(kept + given)
        if number < T - 1:
            state = kept + (given + extended(number))
    return state


def receive(odd, even, low, high):
    space = lax.axis_index("space")

    def take(one, other):
        low[...] = jnp.where(space > 0, one[...], 0.0)
        high[...] = jnp.where(space < S - 1, other[...], 0.0)

    pl.when(space % 2 == 0)(lambda: take(odd, even))
    pl.when(space % 2 == 1)(lambda: take(even, odd))


def chain_rate(below, mob_tile, above):
    return (2.0 * REACTION) * jnp.concatenate([below, mob_tile[...], above], axis=1)


def chain_one_body(terms, mob_tile, odd, even, back, middle, low, high):
    receive(odd, even, low, high)
    extended = chain_parts(terms, [(EARLY, low, high)])
    below, above = early_mobility(low, high)
    rate = chain_rate(below, mob_tile, above)
    weight = around_chain(lax.axis_index("space"), lax.axis_index("tm"))
    back[0] = jnp.zeros((4, CX, 128), jnp.float32)
    state = run_chain(extended(0), extended, rate, weight, range(1, FIRST + 1), back)
    middle[...] = state[:, CX : 2 * CX, :]


def chain_two_body(
    terms, mob_tile, odd, even, late_odd, late_even, first, middle, mid_odd, mid_even,
    back, low, high, late_low, late_high, below, above,
):
    receive(odd, even, low, high)
    receive(late_odd, late_even, late_low, late_high)
    receive(mid_odd, mid_even, below, above)
    late = LATE + (((LAST, 4), (MOBILITY, 4)),)
    extended = chain_parts(terms, [(EARLY, low, high), (late, late_low, late_high)])
    mob_below, mob_above = late_mobility(low, high, late_low, late_high)
    rate = chain_rate(mob_below, mob_tile, mob_above)
    weight = around_chain(lax.axis_index("space"), lax.axis_index("tm"))
    back[pl.ds(0, FIRST + 1)] = first[...]
    state = jnp.concatenate([below[...], middle[...], above[...]], axis=1)
    run_chain(state, extended, rate, weight, range(FIRST + 1, T), back)


def finish_body(fine, coarse_old, arrived, out_far, parts, out, done):
    turn = lax.axis_index("tm")
    lane = iota((CX, 128), 1)
    weight = jnp.where(turn > 0, 1.0, 0.0)
    pick = (iota((256, 256), 0) % 128 == iota((256, 256), 1) // 2).astype(jnp.bfloat16)
    stores = []
    deep = Z // 4
    few, many = deep * CX, deep * X
    chunks = CY // 128
    for group in range(4):
        for part in range(chunks):
            planes = []
            for quarter in range(4):
                total = None
                for k in range(4):
                    block = arrived[4 * part + k, quarter]
                    shift = (OWN * (k - group)) % 128
                    block = pltpu.roll(block, shift, 1) if shift else block
                    total = block if total is None else jnp.where(lane >= OWN * k, block, total)
                planes.append(total)
            advanced = jnp.concatenate(planes, axis=0)
            old = coarse_old[pl.ds(group * few, few), pl.ds(128 * part, 128)]
            both = jnp.concatenate(split(weight * (advanced - old)), axis=1)
            wide = jnp.dot(both, pick, preferred_element_type=jnp.float32)
            for half in range(2):
                block = wide[:, 128 * half : 128 * (half + 1)]
                start = (2 * part + half) * many
                parts[group, pl.ds(start, few, stride=2), :] = block
                parts[group, pl.ds(start + 1, few, stride=2), :] = block
        rows = pl.ds(group * many, many)
        for part in range(2 * chunks):
            columns = pl.ds(128 * part, 128)
            out[rows, columns] = fine[rows, columns] + parts[group, pl.ds(part * many, many), :]
        stores.append(
            pltpu.make_async_copy(out.at[rows, :], out_far.at[rows, :], done.at[group])
        )
        stores[-1].start()
    for store in stores:
        store.wait()


def pack_fine(iterate, mobility):
    rows = jax.ShapeDtypeStruct((3, Z, Y), jnp.float32)
    return pl.pallas_call(
        pack_fine_body,
        out_shape=[rows, rows],
        in_specs=[pl.BlockSpec(memory_space=pltpu.HBM)] * 2,
        out_specs=[pl.BlockSpec(memory_space=pltpu.VMEM)] * 2,
        scratch_shapes=[pltpu.SemaphoreType.DMA((6,))],
        compiler_params=pltpu.CompilerParams(vmem_limit_bytes=PACK_VMEM),
        cost_estimate=pl.CostEstimate(flops=0, bytes_accessed=400_000, transcendentals=0),
    )(iterate, mobility)


def finish(fine, coarse_old, arrived):
    return pl.pallas_call(
        finish_body,
        out_shape=jax.ShapeDtypeStruct((ROWS, Y), jnp.float32),
        in_specs=[pl.BlockSpec(memory_space=pltpu.VMEM)] * 3,
        out_specs=pl.BlockSpec(memory_space=pltpu.HBM),
        scratch_shapes=[
            pltpu.VMEM((4, Y // 128 * X * Z // 4, 128), jnp.float32),
            pltpu.VMEM((ROWS, Y), jnp.float32),
            pltpu.SemaphoreType.DMA((4,)),
        ],
        compiler_params=pltpu.CompilerParams(vmem_limit_bytes=VMEM_LIMIT),
        cost_estimate=pl.CostEstimate(flops=0, bytes_accessed=4_000_000, transcendentals=0),
    )(fine, coarse_old, arrived)


def exchange(odd, even):
    route = []
    for turn in range(T):
        for space in range(S):
            if space in (0, S - 1):
                target = (turn ^ 1) * S + space
            else:
                target = turn * S + space + 2 * (space % 2) - 1
            route.append((turn * S + space, target))
    even_route = [(i, i + 1 - 2 * (i % 2)) for i in range(S)]
    return lax.ppermute(odd, ("tm", "space"), route), lax.ppermute(even, "space", even_route)


def local(iterate, fine_prev, mobility, pending):
    tile = (HALF, CX, 128)
    early = (EARLY_TILES, CX, 128)
    late = (LATE_TILES, CX, 128)
    fields = [field.reshape(ROWS, Y) for field in (iterate, mobility, fine_prev)]
    own_odd, own_even = pack_fine(iterate[0], mobility)
    odd, even = exchange(own_odd, own_even)
    stepped, old_part, mob_tile, outer, flag = call(
        before_body, [(ROWS, Y), (CROWS, CY), tile, (2, Z, Y), (8, 128)], [(Y // 256, ROWS, 128)]
    )(pending.reshape(1, T), fields[0], fields[1])
    fine_part, sent = call(second_body, [(ROWS, Y), (T,) + tile], [(Y // 256, ROWS, 128)])(
        flag, stepped, fields[1], old_part, fields[2]
    )
    sent, change, old_change = call(
        edge_body,
        [(T,) + tile, (2, 2, Z, Y), (2, Z, CY)],
        [(2, 5, Z, Y), (2, T, HALF, 128)],
    )(flag, own_odd, own_even, odd, even, outer, sent)
    terms = lax.all_to_all(sent, "tm", 0, 0)
    odd, even, late_odd, late_even = call(pack_chain_body, [early, early, late, late])(
        terms, mob_tile
    )
    odd, even = exchange(odd, even)
    late_odd, late_even = exchange(late_odd, late_even)
    fine, coarse_old = call(repair_body, [(ROWS, Y), (CROWS, CY)])(
        fine_part, change, old_part, old_change
    )
    odd, even, fine, coarse_old = lax.optimization_barrier((odd, even, fine, coarse_old))
    part = (4, CX, 128)
    first, middle = call(chain_one_body, [(FIRST + 1,) + part, tile], [early, early])(
        terms, mob_tile, odd, even
    )
    mid_odd, mid_even = exchange(middle, middle)
    (back,) = call(chain_two_body, [(T,) + part], [early, early, late, late, tile, tile])(
        terms, mob_tile, odd, even, late_odd, late_even, first, middle, mid_odd, mid_even
    )
    arrived = lax.all_to_all(back, "tm", 0, 0)
    return finish(fine, coarse_old, arrived).reshape(1, Z, X, Y)


def solution(mesh):
    placed = (
        P("tm", None, "space", None),
        P("tm", None, "space", None),
        P(None, "space", None),
        P(),
    )
    return jax.shard_map(
        local, mesh=mesh, in_specs=placed, out_specs=P("tm", None, "space", None), check_vma=False
    )
```

```python
import jax
import jax.numpy as jnp
from jax import lax
from jax.experimental import pallas as pl
from jax.experimental.pallas import tpu as pltpu
from jax.sharding import PartitionSpec as P

Z = 16
X = 16
Y = 1024
T = 16
S = 16
CX = X // 2
CY = Y // 2
ROWS = Z * X
CROWS = Z * CX
OWN = CY // T
MARGIN = 16
HALF = Z // 2
PACKED = 2 * Z + HALF
FIRST = 7
SPAN = 3 * CX

DIFFUSE = 0.15
REACTION = 0.1
VMEM_LIMIT = 48 * 1024 * 1024
PACK_VMEM = 54272 * 1024


MOBILITY = T
EARLY = (
    ((0, 7), (6, 1)),
    ((1, 6), (5, 2)),
    ((2, 5), (4, 3)),
    ((3, 4), (MOBILITY, 4)),
)
LATE = (
    ((8, 7), (14, 1)),
    ((9, 6), (13, 2)),
    ((10, 5), (12, 3)),
)
LAST = 11
EARLY_TILES = len(EARLY) * HALF + 2
LATE_TILES = (len(LATE) + 1) * HALF


def call(body, outs, scratch=(), flops=0):
    return pl.pallas_call(
        body,
        out_shape=[jax.ShapeDtypeStruct(shape, jnp.float32) for shape in outs],
        scratch_shapes=[pltpu.VMEM(shape, jnp.float32) for shape in scratch],
        compiler_params=pltpu.CompilerParams(vmem_limit_bytes=VMEM_LIMIT),
        cost_estimate=pl.CostEstimate(flops=flops, bytes_accessed=4_000_000, transcendentals=0),
    )


def iota(shape, axis):
    return lax.broadcasted_iota(jnp.int32, shape, axis)


def split(value):
    high = value.astype(jnp.bfloat16)
    low = (value - high.astype(jnp.float32)).astype(jnp.bfloat16)
    return high, low


def restrict(value, parts):
    high, low = split(value)
    pick = (iota((256, 128), 0) // 2 == iota((256, 128), 1)).astype(jnp.bfloat16)
    for k in range(Y // 256):
        chunk = slice(256 * k, 256 * (k + 1))
        parts[k] = jnp.dot(high[:, chunk], pick, preferred_element_type=jnp.float32) + jnp.dot(
            low[:, chunk], pick, preferred_element_type=jnp.float32
        )
    pieces = [
        parts[k, pl.ds(0, CROWS, stride=2), :] + parts[k, pl.ds(1, CROWS, stride=2), :]
        for k in range(Y // 256)
    ]
    return 0.25 * jnp.concatenate(pieces, axis=1)


def halve_lanes(value):
    high, low = split(value)
    pick = (iota((256, 128), 0) // 2 == iota((256, 128), 1)).astype(jnp.bfloat16)
    pieces = []
    for k in range(Y // 256):
        chunk = slice(256 * k, 256 * (k + 1))
        pieces.append(
            jnp.dot(high[:, chunk], pick, preferred_element_type=jnp.float32)
            + jnp.dot(low[:, chunk], pick, preferred_element_type=jnp.float32)
        )
    return jnp.concatenate(pieces, axis=1)


def beside_lanes(value):
    count = value.shape[-1]
    axis = value.ndim - 1
    before = pltpu.roll(value, 1, axis)
    after = pltpu.roll(value, count - 1, axis)
    lane = iota(value.shape[:-1] + (128,), axis)
    before = jnp.concatenate(
        [jnp.where(lane == 0, 0.0, before[..., :128]), before[..., 128:]], axis=axis
    )
    after = jnp.concatenate(
        [after[..., :-128], jnp.where(lane == 127, 0.0, after[..., -128:])], axis=axis
    )
    return before + after


def fine_rule(center, around, mobility):
    return DIFFUSE * around + REACTION * (center * (1.0 + mobility * (1.0 - center * center)))


def fine_tile(ref, mob_ref, z, tile, low_row, high_row):
    base = z * X + tile * 8
    center = ref[pl.ds(base, 8), :]
    row = iota((8, Y), 0)
    below = ref[pl.ds(base - 1, 1), :] if tile else low_row
    above = high_row if tile else ref[pl.ds(base + 8, 1), :]
    around = jnp.where(row == 0, below, pltpu.roll(center, 1, 0))
    around += jnp.where(row == 7, above, pltpu.roll(center, 7, 0))
    around += beside_lanes(center)
    if z > 0:
        around += ref[pl.ds(base - X, 8), :]
    if z < Z - 1:
        around += ref[pl.ds(base + X, 8), :]
    return fine_rule(center, around, mob_ref[pl.ds(base, 8), :])


def pack_fine_body(iterate, mobility, odd, even, own_mob, rows, done):
    space = lax.axis_index("space")
    ends = ((0, 1), (X - 1, X - 2))
    moves = []
    for side, (near, far) in enumerate(ends):
        for source, inner, target in (
            (iterate, near, rows.at[side, 0]),
            (iterate, far, rows.at[side, 1]),
            (mobility, near, own_mob.at[side]),
        ):
            moves.append(
                pltpu.make_async_copy(source.at[:, inner, :], target, done.at[len(moves)])
            )
    for move in moves:
        move.start()
    for move in moves:
        move.wait()
    sums = [rows[side, 0] + rows[side, 1] for side in range(2)]
    halved = halve_lanes(jnp.concatenate(sums, axis=0))

    def put(low, high):
        for side, out in enumerate((low, high)):
            near, far = rows[side, 0], rows[side, 1]
            out[pl.ds(0, Z), :] = near
            out[pl.ds(Z, Z), :] = fine_rule(near, far, own_mob[side])
            coarse = halved[side * Z : (side + 1) * Z]
            out[pl.ds(2 * Z, HALF), pl.ds(0, CY)] = coarse[:HALF]
            out[pl.ds(2 * Z, HALF), pl.ds(CY, CY)] = coarse[HALF:]

    pl.when(space % 2 == 0)(lambda: put(odd, even))
    pl.when(space % 2 == 1)(lambda: put(even, odd))


def windows(value):
    count = CY // 128
    blank = jnp.zeros((HALF, CX, 128), jnp.float32)
    lane = iota((HALF, CX, 128), 2)
    moved = {}

    def piece(half, index, amount):
        if not 0 <= index < count:
            return blank
        if (half, index, amount) not in moved:
            planes = value[HALF * half : HALF * (half + 1)]
            moved[half, index, amount] = pltpu.roll(
                planes[:, :, 128 * index : 128 * (index + 1)], amount, 2
            )
        return moved[half, index, amount]

    tiles = []
    for tile in range(T):
        start = tile * OWN - MARGIN
        first = start // 128
        offset = start - first * 128
        parts = []
        for half in range(2):
            amount = (64 * half - offset) % 128
            part = piece(half, first, amount)
            if offset + 64 > 128:
                after = piece(half, first + 1, amount)
                part = jnp.where(lane < 64 * half + 128 - offset, part, after)
            parts.append(part)
        tiles.append(jnp.where(lane < 64, parts[0], parts[1]))
    return tiles


def turned(value, tile):
    start = tile * OWN - MARGIN
    wide = jnp.concatenate([value, jnp.zeros((Z, CX, 128), jnp.float32)], axis=2)
    count = CY + 128
    first = pltpu.roll(wide[:HALF], (count - start) % count, 2)[:, :, :128]
    second = pltpu.roll(wide[HALF:], (count - start + 64) % count, 2)[:, :, :128]
    return jnp.where(iota((HALF, CX, 128), 2) < 64, first, second)


def partial_step(source, mobility, target):
    none = jnp.zeros((1, Y), jnp.float32)
    for z in range(Z):
        for tile in range(X // 8):
            target[pl.ds(z * X + tile * 8, 8), :] = fine_tile(
                source, mobility, z, tile, none, none
            )


def before_body(pending, iterate, mobility, stepped, coarse_old, mob_tile, outer, flag, parts):
    turn = lax.axis_index("tm")
    mine = jnp.where(iota((1, T), 1) == turn, pending[...], 0)
    chosen = jnp.sum(mine, axis=1, keepdims=True)
    flag[...] = jnp.broadcast_to(jnp.where(chosen > 0, 1.0, 0.0), (8, 128))
    partial_step(iterate, mobility, stepped)
    for side, inner in ((0, 0), (1, X - 1)):
        for z in range(Z):
            outer[side, pl.ds(z, 1), :] = stepped[pl.ds(z * X + inner, 1), :]
    coarse_mobility = restrict(mobility[...], parts).reshape(Z, CX, CY)
    start = restrict(iterate[...], parts).reshape(Z, CX, CY)
    row = iota((Z, CX, CY), 1)
    around = jnp.where(row == 0, 0.0, pltpu.roll(start, 1, 1))
    around += jnp.where(row == CX - 1, 0.0, pltpu.roll(start, CX - 1, 1))
    around += beside_lanes(start)
    flat = jnp.zeros((1, CX, CY), jnp.float32)
    stacked = jnp.concatenate([start[1:], flat], axis=0)
    stacked += jnp.concatenate([flat, start[:-1]], axis=0)
    rate = 2.0 * REACTION * coarse_mobility
    kept, given = coarse_rule(start, 0.5 * DIFFUSE * around, stacked, rate)
    coarse_old[...] = (kept + given).reshape(CROWS, CY)
    mob_tile[...] = turned(coarse_mobility, turn)


def second_body(flag, stepped, mobility, coarse_old, previous, fine, sent, parts):
    turn = lax.axis_index("tm")
    flagged = jnp.max(flag[...]) > 0.5
    pl.when(flagged)(lambda: partial_step(stepped, mobility, fine))

    @pl.when(jnp.logical_not(flagged))
    def _():
        fine[...] = previous[...]

    weight = jnp.where(turn > 0, 1.0, 0.0)
    term = restrict(fine[...], parts) - weight * coarse_old[...]
    for tile, value in enumerate(windows(term.reshape(Z, CX, CY))):
        sent[tile] = value


def coarse_rule(center, beside, stacked, rate):
    bottom = 1.0 + rate * (center * center)
    inverse = pltpu.reciprocal(bottom, approx=True)
    inverse = inverse * (2.0 - bottom * inverse)
    kept = center * ((1.0 + rate) * inverse - 6.0 * DIFFUSE)
    return kept, beside + 2.0 * DIFFUSE * stacked


def edge_windows(value):
    count = CY // 128
    lane = iota((HALF, 128), 1)
    moved = {}

    def piece(half, index, amount):
        if not 0 <= index < count:
            return jnp.zeros((HALF, 128), jnp.float32)
        if (half, index, amount) not in moved:
            part = value[HALF * half : HALF * (half + 1), 128 * index : 128 * (index + 1)]
            moved[half, index, amount] = pltpu.roll(part, amount, 1)
        return moved[half, index, amount]

    tiles = []
    for tile in range(T):
        start = tile * OWN - MARGIN
        first = start // 128
        offset = start - first * 128
        parts = []
        for half in range(2):
            amount = (64 * half - offset) % 128
            part = piece(half, first, amount)
            if offset + 64 > 128:
                after = piece(half, first + 1, amount)
                part = jnp.where(lane < 64 * half + 128 - offset, part, after)
            parts.append(part)
        tiles.append(jnp.where(lane < 64, parts[0], parts[1]))
    return tiles


def edge_body(
    flag, own_odd, own_even, odd, even, own_mob, outer, sent_in,
    sent, change, old_change, halo, added_rows,
):
    space = lax.axis_index("space")
    turn = lax.axis_index("tm")

    def take(low, high, own_low, own_high):
        for side, (got, own) in enumerate(((low, own_low), (high, own_high))):
            halo[side, pl.ds(0, PACKED), :] = got[...]
            halo[side, pl.ds(PACKED, Z), :] = own[pl.ds(0, Z), :]

    pl.when(space % 2 == 0)(lambda: take(odd, even, own_odd, own_even))
    pl.when(space % 2 == 1)(lambda: take(even, odd, own_even, own_odd))

    flagged = flag[pl.ds(0, 1), pl.ds(0, 1)]
    weight = jnp.where(turn > 0, 1.0, 0.0)
    plane = iota((Z, Y), 0)

    def beside(value):
        total = jnp.where(plane == 0, 0.0, pltpu.roll(value, 1, 0))
        total += jnp.where(plane == Z - 1, 0.0, pltpu.roll(value, Z - 1, 0))
        return total + beside_lanes(value)

    sums, coarse_sides = [], []
    for side, inside in ((0, space > 0), (1, space < S - 1)):
        keep = jnp.where(inside, 1.0, 0.0)
        near, given = keep * halo[side, pl.ds(0, Z), :], halo[side, pl.ds(Z, Z), :]
        own, own_mobility = halo[side, pl.ds(PACKED, Z), :], own_mob[side]
        beyond = keep * (given + DIFFUSE * (own + beside(near)))
        planes = pl.ds(2 * Z, HALF)
        coarse = [halo[side, planes, pl.ds(half * CY, CY)] for half in range(2)]
        coarse_sides.append((keep * 0.5 * DIFFUSE * 0.25) * jnp.concatenate(coarse, axis=0))
        added = DIFFUSE * near
        before = outer[side]
        after = before + added
        grown = after * (1.0 - after * after) - before * (1.0 - before * before)
        first = added + DIFFUSE * (beyond + beside(added) - 6.0 * added)
        first = flagged * (first + REACTION * own_mobility * grown)
        second = flagged * DIFFUSE * added
        change[side, 0] = first
        change[side, 1] = second
        sums.append(first + second)
    halved = halve_lanes(jnp.concatenate(sums, axis=0))
    for side in range(2):
        coarse_side = coarse_sides[side]
        fine_side = 0.25 * halved[side * Z : (side + 1) * Z]
        old_change[side] = coarse_side
        for tile, value in enumerate(edge_windows(fine_side - weight * coarse_side)):
            added_rows[side, tile] = value
    row = iota((CX, 128), 0)
    for tile in range(T):
        for z in range(HALF):
            low = added_rows[0, tile, pl.ds(z, 1), :]
            high = added_rows[1, tile, pl.ds(z, 1), :]
            change_here = jnp.where(row == 0, low, jnp.where(row == CX - 1, high, 0.0))
            sent[tile, z] = sent_in[tile, z] + change_here


def repair_body(fine_in, change, old_in, old_change, fine, coarse_old):
    row = iota((8, Y), 0)
    coarse_row = iota((CX, CY), 0)
    for z in range(Z):
        for side in range(2):
            here = pl.ds(z * X + side * 8, 8)
            first = change[side, 0, pl.ds(z, 1), :]
            second = change[side, 1, pl.ds(z, 1), :]
            last = 7 * side
            added = jnp.where(row == last, first, jnp.where(row == abs(last - 1), second, 0.0))
            fine[here, :] = fine_in[here, :] + added
        here = pl.ds(z * CX, CX)
        low, high = old_change[0, pl.ds(z, 1), :], old_change[1, pl.ds(z, 1), :]
        added = jnp.where(coarse_row == 0, low, jnp.where(coarse_row == CX - 1, high, 0.0))
        coarse_old[here, :] = old_in[here, :] + added


def pack_chain_body(terms, mob_tile, odd, even, late_odd, late_even):
    space = lax.axis_index("space")
    row = iota((HALF, CX, 128), 1)

    def of(number):
        return mob_tile[...] if number == MOBILITY else terms[number]

    def put(low, high, late_low, late_high):
        for pairs, first, last in ((EARLY, low, high), (LATE, late_low, late_high)):
            for k, ((one, rows), (other, rest)) in enumerate(pairs):
                here, there = of(one), of(other)
                place = pl.ds(k * HALF, HALF)
                first[place] = jnp.where(row < rows, here, pltpu.roll(there, rows, 1))
                last[place] = jnp.where(row >= rest, here, pltpu.roll(there, rest, 1))
        for k in range(2):
            for z in range(HALF):
                low[EARLY_TILES - 2 + k, pl.ds(z, 1), :] = mob_tile[z, pl.ds(4 + k, 1), :]
                high[EARLY_TILES - 2 + k, pl.ds(z, 1), :] = mob_tile[z, pl.ds(2 + k, 1), :]
        place = pl.ds(len(LATE) * HALF, HALF)
        late_low[place] = jnp.where(row < 4, terms[LAST], mob_tile[...])
        late_high[place] = jnp.where(row >= 4, terms[LAST], mob_tile[...])

    pl.when(space % 2 == 0)(lambda: put(odd, even, late_odd, late_even))
    pl.when(space % 2 == 1)(lambda: put(even, odd, late_even, late_odd))


def chain_parts(terms, shipments):
    place = {}
    for pairs, low, high in shipments:
        for k, ((one, rows), (other, rest)) in enumerate(pairs):
            place[one] = (low, high, k, 0, 0)
            place[other] = (low, high, k, CX - rest, CX - rows)

    def extended(number):
        own = terms[number]
        if number not in place:
            return jnp.concatenate([jnp.zeros_like(own), own, jnp.zeros_like(own)], axis=1)
        low, high, k, up, down = place[number]
        below, above = low[pl.ds(k * HALF, HALF)], high[pl.ds(k * HALF, HALF)]
        if up:
            below = pltpu.roll(below, up, 1)
            above = pltpu.roll(above, down, 1)
        return jnp.concatenate([below, own, above], axis=1)

    return extended


def inner_mobility(low, high):
    place = pl.ds((len(EARLY) - 1) * HALF, HALF)
    return pltpu.roll(low[place], 4, 1), pltpu.roll(high[place], 4, 1)


def early_mobility(low, high):
    below, above = inner_mobility(low, high)
    row = iota((CX, 128), 0)
    lows, highs = [], []
    for z in range(HALF):
        low_rows = [low[EARLY_TILES - 2 + k, pl.ds(z, 1), :] for k in range(2)]
        high_rows = [high[EARLY_TILES - 2 + k, pl.ds(z, 1), :] for k in range(2)]
        outer = jnp.where(row == 2, low_rows[0], jnp.where(row == 3, low_rows[1], 0.0))
        lows.append(jnp.where(row >= 4, below[z], outer)[None])
        outer = jnp.where(row == 4, high_rows[0], jnp.where(row == 5, high_rows[1], 0.0))
        highs.append(jnp.where(row < 4, above[z], outer)[None])
    return jnp.concatenate(lows, axis=0), jnp.concatenate(highs, axis=0)


def late_mobility(low, high, late_low, late_high):
    below, above = inner_mobility(low, high)
    place = pl.ds(len(LATE) * HALF, HALF)
    row = iota((HALF, CX, 128), 1)
    return (
        jnp.where(row >= 4, below, late_low[place]),
        jnp.where(row < 4, above, late_high[place]),
    )


def around_chain(space, turn):
    row = iota((1, SPAN, 128), 1) - CX + space * CX
    column = iota((1, SPAN, 128), 2) % 64 - MARGIN + turn * OWN
    inside = (row >= 0) & (row < S * CX) & (column >= 0) & (column < CY)
    return jnp.where(inside, 0.5 * DIFFUSE, 0.0)


def chain_step(state, rate, weight):
    lane = iota((1, SPAN, 128), 2)
    crossed_up = jnp.where(lane < 64, pltpu.roll(state[:1], 64, 2), 0.0)
    crossed_down = jnp.where(lane >= 64, pltpu.roll(state[HALF - 1 :], 64, 2), 0.0)
    stacked = jnp.concatenate([state[1:], crossed_up], axis=0)
    stacked += jnp.concatenate([crossed_down, state[:-1]], axis=0)
    beside = pltpu.roll(state, 1, 1) + pltpu.roll(state, SPAN - 1, 1)
    beside += pltpu.roll(state, 1, 2) + pltpu.roll(state, 127, 2)
    return coarse_rule(state, weight * beside, stacked, rate)


def returned(advanced):
    own = advanced[:, CX : 2 * CX, :]
    lane = iota((4, CX, 128), 2)
    return jnp.where(
        lane % 64 < OWN,
        pltpu.roll(own[:4], 128 - MARGIN, 2),
        pltpu.roll(own[4:], OWN - MARGIN, 2),
    )


def run_chain(state, extended, rate, weight, numbers, back):
    for number in numbers:
        kept, given = chain_step(state, rate, weight)
        back[number] = returned(kept + given)
        if number < T - 1:
            state = kept + (given + extended(number))
    return state


def receive(odd, even, low, high):
    space = lax.axis_index("space")

    def take(one, other):
        low[...] = jnp.where(space > 0, one[...], 0.0)
        high[...] = jnp.where(space < S - 1, other[...], 0.0)

    pl.when(space % 2 == 0)(lambda: take(odd, even))
    pl.when(space % 2 == 1)(lambda: take(even, odd))


def chain_rate(below, mob_tile, above):
    return (2.0 * REACTION) * jnp.concatenate([below, mob_tile[...], above], axis=1)


def chain_one_body(terms, mob_tile, odd, even, back, middle, low, high):
    receive(odd, even, low, high)
    extended = chain_parts(terms, [(EARLY, low, high)])
    below, above = early_mobility(low, high)
    rate = chain_rate(below, mob_tile, above)
    weight = around_chain(lax.axis_index("space"), lax.axis_index("tm"))
    back[0] = jnp.zeros((4, CX, 128), jnp.float32)
    state = run_chain(extended(0), extended, rate, weight, range(1, FIRST + 1), back)
    middle[...] = state[:, CX : 2 * CX, :]


def chain_two_body(
    terms, mob_tile, odd, even, late_odd, late_even, first, middle, mid_odd, mid_even,
    back, low, high, late_low, late_high, below, above,
):
    receive(odd, even, low, high)
    receive(late_odd, late_even, late_low, late_high)
    receive(mid_odd, mid_even, below, above)
    late = LATE + (((LAST, 4), (MOBILITY, 4)),)
    extended = chain_parts(terms, [(EARLY, low, high), (late, late_low, late_high)])
    mob_below, mob_above = late_mobility(low, high, late_low, late_high)
    rate = chain_rate(mob_below, mob_tile, mob_above)
    weight = around_chain(lax.axis_index("space"), lax.axis_index("tm"))
    back[pl.ds(0, FIRST + 1)] = first[...]
    state = jnp.concatenate([below[...], middle[...], above[...]], axis=1)
    run_chain(state, extended, rate, weight, range(FIRST + 1, T), back)


def finish_body(fine, coarse_old, arrived, out_far, parts, out, done):
    turn = lax.axis_index("tm")
    lane = iota((CX, 128), 1)
    weight = jnp.where(turn > 0, 1.0, 0.0)
    pick = (iota((256, 256), 0) % 128 == iota((256, 256), 1) // 2).astype(jnp.bfloat16)
    stores = []
    deep = Z // 4
    few, many = deep * CX, deep * X
    chunks = CY // 128
    for group in range(4):
        for part in range(chunks):
            planes = []
            for quarter in range(4):
                total = None
                for k in range(4):
                    block = arrived[4 * part + k, quarter]
                    shift = (OWN * (k - group)) % 128
                    block = pltpu.roll(block, shift, 1) if shift else block
                    total = block if total is None else jnp.where(lane >= OWN * k, block, total)
                planes.append(total)
            advanced = jnp.concatenate(planes, axis=0)
            old = coarse_old[pl.ds(group * few, few), pl.ds(128 * part, 128)]
            both = jnp.concatenate(split(weight * (advanced - old)), axis=1)
            wide = jnp.dot(both, pick, preferred_element_type=jnp.float32)
            for half in range(2):
                block = wide[:, 128 * half : 128 * (half + 1)]
                start = (2 * part + half) * many
                parts[group, pl.ds(start, few, stride=2), :] = block
                parts[group, pl.ds(start + 1, few, stride=2), :] = block
        rows = pl.ds(group * many, many)
        for part in range(2 * chunks):
            columns = pl.ds(128 * part, 128)
            out[rows, columns] = fine[rows, columns] + parts[group, pl.ds(part * many, many), :]
        stores.append(
            pltpu.make_async_copy(out.at[rows, :], out_far.at[rows, :], done.at[group])
        )
        stores[-1].start()
    for store in stores:
        store.wait()


def pack_fine(iterate, mobility):
    outs = [(PACKED, Y), (PACKED, Y), (2, Z, Y)]
    return pl.pallas_call(
        pack_fine_body,
        out_shape=[jax.ShapeDtypeStruct(shape, jnp.float32) for shape in outs],
        in_specs=[pl.BlockSpec(memory_space=pltpu.HBM)] * 2,
        out_specs=[pl.BlockSpec(memory_space=pltpu.VMEM)] * 3,
        scratch_shapes=[pltpu.VMEM((2, 2, Z, Y), jnp.float32), pltpu.SemaphoreType.DMA((6,))],
        compiler_params=pltpu.CompilerParams(vmem_limit_bytes=PACK_VMEM),
        cost_estimate=pl.CostEstimate(flops=0, bytes_accessed=400_000, transcendentals=0),
    )(iterate, mobility)


def finish(fine, coarse_old, arrived):
    return pl.pallas_call(
        finish_body,
        out_shape=jax.ShapeDtypeStruct((ROWS, Y), jnp.float32),
        in_specs=[pl.BlockSpec(memory_space=pltpu.VMEM)] * 3,
        out_specs=pl.BlockSpec(memory_space=pltpu.HBM),
        scratch_shapes=[
            pltpu.VMEM((4, Y // 128 * X * Z // 4, 128), jnp.float32),
            pltpu.VMEM((ROWS, Y), jnp.float32),
            pltpu.SemaphoreType.DMA((4,)),
        ],
        compiler_params=pltpu.CompilerParams(vmem_limit_bytes=VMEM_LIMIT),
        cost_estimate=pl.CostEstimate(flops=0, bytes_accessed=4_000_000, transcendentals=0),
    )(fine, coarse_old, arrived)


def exchange(odd, even):
    route = []
    for turn in range(T):
        for space in range(S):
            if space in (0, S - 1):
                target = (turn ^ 1) * S + space
            else:
                target = turn * S + space + 2 * (space % 2) - 1
            route.append((turn * S + space, target))
    even_route = [(i, i + 1 - 2 * (i % 2)) for i in range(S)]
    return lax.ppermute(odd, ("tm", "space"), route), lax.ppermute(even, "space", even_route)


def local(iterate, fine_prev, mobility, pending):
    tile = (HALF, CX, 128)
    early = (EARLY_TILES, CX, 128)
    late = (LATE_TILES, CX, 128)
    fields = [field.reshape(ROWS, Y) for field in (iterate, mobility, fine_prev)]
    own_odd, own_even, own_mob = pack_fine(iterate[0], mobility)
    odd, even = exchange(own_odd, own_even)
    stepped, old_part, mob_tile, outer, flag = call(
        before_body, [(ROWS, Y), (CROWS, CY), tile, (2, Z, Y), (8, 128)], [(Y // 256, ROWS, 128)]
    )(pending.reshape(1, T), fields[0], fields[1])
    fine_part, sent = call(second_body, [(ROWS, Y), (T,) + tile], [(Y // 256, ROWS, 128)])(
        flag, stepped, fields[1], old_part, fields[2]
    )
    sent, change, old_change = call(
        edge_body,
        [(T,) + tile, (2, 2, Z, Y), (2, Z, CY)],
        [(2, PACKED + Z, Y), (2, T, HALF, 128)],
    )(flag, own_odd, own_even, odd, even, own_mob, outer, sent)
    terms = lax.all_to_all(sent, "tm", 0, 0)
    odd, even, late_odd, late_even = call(pack_chain_body, [early, early, late, late])(
        terms, mob_tile
    )
    odd, even = exchange(odd, even)
    late_odd, late_even = exchange(late_odd, late_even)
    fine, coarse_old = call(repair_body, [(ROWS, Y), (CROWS, CY)])(
        fine_part, change, old_part, old_change
    )
    odd, even, fine, coarse_old = lax.optimization_barrier((odd, even, fine, coarse_old))
    part = (4, CX, 128)
    first, middle = call(chain_one_body, [(FIRST + 1,) + part, tile], [early, early])(
        terms, mob_tile, odd, even
    )
    mid_odd, mid_even = exchange(middle, middle)
    (back,) = call(chain_two_body, [(T,) + part], [early, early, late, late, tile, tile])(
        terms, mob_tile, odd, even, late_odd, late_even, first, middle, mid_odd, mid_even
    )
    arrived = lax.all_to_all(back, "tm", 0, 0)
    return finish(fine, coarse_old, arrived).reshape(1, Z, X, Y)


def solution(mesh):
    placed = (
        P("tm", None, "space", None),
        P("tm", None, "space", None),
        P(None, "space", None),
        P(),
    )
    return jax.shard_map(
        local, mesh=mesh, in_specs=placed, out_specs=P("tm", None, "space", None), check_vma=False
    )
```

```python
import jax
import jax.numpy as jnp
from jax import lax
from jax.experimental import pallas as pl
from jax.experimental.pallas import tpu as pltpu
from jax.sharding import PartitionSpec as P

Z = 16
X = 16
Y = 1024
T = 16
S = 16
CX = X // 2
CY = Y // 2
ROWS = Z * X
CROWS = Z * CX
OWN = CY // T
MARGIN = 16
HALF = Z // 2
FIRST = 7
SPAN = 3 * CX

DIFFUSE = 0.15
REACTION = 0.1
VMEM_LIMIT = 48 * 1024 * 1024
PACK_VMEM = 54272 * 1024


MOBILITY = T
EARLY = (
    ((0, 7), (6, 1)),
    ((1, 6), (5, 2)),
    ((2, 5), (4, 3)),
    ((3, 4), (MOBILITY, 4)),
)
LATE = (
    ((8, 7), (14, 1)),
    ((9, 6), (13, 2)),
    ((10, 5), (12, 3)),
)
LAST = 11
EARLY_TILES = len(EARLY) * HALF + 2
LATE_TILES = (len(LATE) + 1) * HALF


def call(body, outs, scratch=(), flops=0):
    return pl.pallas_call(
        body,
        out_shape=[jax.ShapeDtypeStruct(shape, jnp.float32) for shape in outs],
        scratch_shapes=[pltpu.VMEM(shape, jnp.float32) for shape in scratch],
        compiler_params=pltpu.CompilerParams(vmem_limit_bytes=VMEM_LIMIT),
        cost_estimate=pl.CostEstimate(flops=flops, bytes_accessed=4_000_000, transcendentals=0),
    )


def iota(shape, axis):
    return lax.broadcasted_iota(jnp.int32, shape, axis)


def split(value):
    high = value.astype(jnp.bfloat16)
    low = (value - high.astype(jnp.float32)).astype(jnp.bfloat16)
    return high, low


def restrict(value, parts):
    high, low = split(value)
    pick = (iota((256, 128), 0) // 2 == iota((256, 128), 1)).astype(jnp.bfloat16)
    for k in range(Y // 256):
        chunk = slice(256 * k, 256 * (k + 1))
        parts[k] = jnp.dot(high[:, chunk], pick, preferred_element_type=jnp.float32) + jnp.dot(
            low[:, chunk], pick, preferred_element_type=jnp.float32
        )
    pieces = [
        parts[k, pl.ds(0, CROWS, stride=2), :] + parts[k, pl.ds(1, CROWS, stride=2), :]
        for k in range(Y // 256)
    ]
    return 0.25 * jnp.concatenate(pieces, axis=1)


def halve_lanes(value):
    high, low = split(value)
    pick = (iota((256, 128), 0) // 2 == iota((256, 128), 1)).astype(jnp.bfloat16)
    pieces = []
    for k in range(Y // 256):
        chunk = slice(256 * k, 256 * (k + 1))
        pieces.append(
            jnp.dot(high[:, chunk], pick, preferred_element_type=jnp.float32)
            + jnp.dot(low[:, chunk], pick, preferred_element_type=jnp.float32)
        )
    return jnp.concatenate(pieces, axis=1)


def beside_lanes(value):
    count = value.shape[-1]
    axis = value.ndim - 1
    before = pltpu.roll(value, 1, axis)
    after = pltpu.roll(value, count - 1, axis)
    lane = iota(value.shape[:-1] + (128,), axis)
    before = jnp.concatenate(
        [jnp.where(lane == 0, 0.0, before[..., :128]), before[..., 128:]], axis=axis
    )
    after = jnp.concatenate(
        [after[..., :-128], jnp.where(lane == 127, 0.0, after[..., -128:])], axis=axis
    )
    return before + after


def fine_rule(center, around, mobility):
    return DIFFUSE * around + REACTION * (center * (1.0 + mobility * (1.0 - center * center)))


def fine_tile(ref, mob_ref, z, tile, low_row, high_row):
    base = z * X + tile * 8
    center = ref[pl.ds(base, 8), :]
    row = iota((8, Y), 0)
    below = ref[pl.ds(base - 1, 1), :] if tile else low_row
    above = high_row if tile else ref[pl.ds(base + 8, 1), :]
    around = jnp.where(row == 0, below, pltpu.roll(center, 1, 0))
    around += jnp.where(row == 7, above, pltpu.roll(center, 7, 0))
    around += beside_lanes(center)
    if z > 0:
        around += ref[pl.ds(base - X, 8), :]
    if z < Z - 1:
        around += ref[pl.ds(base + X, 8), :]
    return fine_rule(center, around, mob_ref[pl.ds(base, 8), :])


def pack_fine_body(iterate, mobility, odd, even, done):
    space = lax.axis_index("space")

    def put(low, high):
        moves = []
        for out, near, far in ((low, 0, 1), (high, X - 1, X - 2)):
            for k, (source, inner) in enumerate(((iterate, near), (iterate, far), (mobility, near))):
                moves.append(
                    pltpu.make_async_copy(source.at[:, inner, :], out.at[k], done.at[len(moves)])
                )
        for move in moves:
            move.start()
        for move in moves:
            move.wait()

    pl.when(space % 2 == 0)(lambda: put(odd, even))
    pl.when(space % 2 == 1)(lambda: put(even, odd))


def windows(value):
    count = CY // 128
    blank = jnp.zeros((HALF, CX, 128), jnp.float32)
    lane = iota((HALF, CX, 128), 2)
    moved = {}

    def piece(half, index, amount):
        if not 0 <= index < count:
            return blank
        if (half, index, amount) not in moved:
            planes = value[HALF * half : HALF * (half + 1)]
            moved[half, index, amount] = pltpu.roll(
                planes[:, :, 128 * index : 128 * (index + 1)], amount, 2
            )
        return moved[half, index, amount]

    tiles = []
    for tile in range(T):
        start = tile * OWN - MARGIN
        first = start // 128
        offset = start - first * 128
        parts = []
        for half in range(2):
            amount = (64 * half - offset) % 128
            part = piece(half, first, amount)
            if offset + 64 > 128:
                after = piece(half, first + 1, amount)
                part = jnp.where(lane < 64 * half + 128 - offset, part, after)
            parts.append(part)
        tiles.append(jnp.where(lane < 64, parts[0], parts[1]))
    return tiles


def turned(value, tile):
    start = tile * OWN - MARGIN
    wide = jnp.concatenate([value, jnp.zeros((Z, CX, 128), jnp.float32)], axis=2)
    count = CY + 128
    first = pltpu.roll(wide[:HALF], (count - start) % count, 2)[:, :, :128]
    second = pltpu.roll(wide[HALF:], (count - start + 64) % count, 2)[:, :, :128]
    return jnp.where(iota((HALF, CX, 128), 2) < 64, first, second)


def partial_step(source, mobility, target):
    none = jnp.zeros((1, Y), jnp.float32)
    for z in range(Z):
        for tile in range(X // 8):
            target[pl.ds(z * X + tile * 8, 8), :] = fine_tile(
                source, mobility, z, tile, none, none
            )


def before_body(pending, iterate, mobility, stepped, coarse_old, mob_tile, outer, flag, parts):
    turn = lax.axis_index("tm")
    mine = jnp.where(iota((1, T), 1) == turn, pending[...], 0)
    chosen = jnp.sum(mine, axis=1, keepdims=True)
    flag[...] = jnp.broadcast_to(jnp.where(chosen > 0, 1.0, 0.0), (8, 128))
    partial_step(iterate, mobility, stepped)
    for side, inner in ((0, 0), (1, X - 1)):
        for z in range(Z):
            outer[side, pl.ds(z, 1), :] = stepped[pl.ds(z * X + inner, 1), :]
    coarse_mobility = restrict(mobility[...], parts).reshape(Z, CX, CY)
    start = restrict(iterate[...], parts).reshape(Z, CX, CY)
    row = iota((Z, CX, CY), 1)
    around = jnp.where(row == 0, 0.0, pltpu.roll(start, 1, 1))
    around += jnp.where(row == CX - 1, 0.0, pltpu.roll(start, CX - 1, 1))
    around += beside_lanes(start)
    flat = jnp.zeros((1, CX, CY), jnp.float32)
    stacked = jnp.concatenate([start[1:], flat], axis=0)
    stacked += jnp.concatenate([flat, start[:-1]], axis=0)
    rate = 2.0 * REACTION * coarse_mobility
    kept, given = coarse_rule(start, 0.5 * DIFFUSE * around, stacked, rate)
    coarse_old[...] = (kept + given).reshape(CROWS, CY)
    mob_tile[...] = turned(coarse_mobility, turn)


def second_body(flag, stepped, mobility, coarse_old, previous, fine, sent, parts):
    turn = lax.axis_index("tm")
    flagged = jnp.max(flag[...]) > 0.5
    pl.when(flagged)(lambda: partial_step(stepped, mobility, fine))

    @pl.when(jnp.logical_not(flagged))
    def _():
        fine[...] = previous[...]

    weight = jnp.where(turn > 0, 1.0, 0.0)
    term = restrict(fine[...], parts) - weight * coarse_old[...]
    for tile, value in enumerate(windows(term.reshape(Z, CX, CY))):
        sent[tile] = value


def coarse_rule(center, beside, stacked, rate):
    bottom = 1.0 + rate * (center * center)
    inverse = pltpu.reciprocal(bottom, approx=True)
    inverse = inverse * (2.0 - bottom * inverse)
    kept = center * ((1.0 + rate) * inverse - 6.0 * DIFFUSE)
    return kept, beside + 2.0 * DIFFUSE * stacked


def edge_windows(value):
    count = CY // 128
    lane = iota((HALF, 128), 1)
    moved = {}

    def piece(half, index, amount):
        if not 0 <= index < count:
            return jnp.zeros((HALF, 128), jnp.float32)
        if (half, index, amount) not in moved:
            part = value[HALF * half : HALF * (half + 1), 128 * index : 128 * (index + 1)]
            moved[half, index, amount] = pltpu.roll(part, amount, 1)
        return moved[half, index, amount]

    tiles = []
    for tile in range(T):
        start = tile * OWN - MARGIN
        first = start // 128
        offset = start - first * 128
        parts = []
        for half in range(2):
            amount = (64 * half - offset) % 128
            part = piece(half, first, amount)
            if offset + 64 > 128:
                after = piece(half, first + 1, amount)
                part = jnp.where(lane < 64 * half + 128 - offset, part, after)
            parts.append(part)
        tiles.append(jnp.where(lane < 64, parts[0], parts[1]))
    return tiles


def edge_body(
    flag, own_odd, own_even, odd, even, outer, sent_in, sent, change, old_change, added_rows
):
    space = lax.axis_index("space")
    turn = lax.axis_index("tm")

    def run(*sides):
        flagged = flag[pl.ds(0, 1), pl.ds(0, 1)]
        weight = jnp.where(turn > 0, 1.0, 0.0)
        plane = iota((Z, Y), 0)

        def beside(value):
            total = jnp.where(plane == 0, 0.0, pltpu.roll(value, 1, 0))
            total += jnp.where(plane == Z - 1, 0.0, pltpu.roll(value, Z - 1, 0))
            return total + beside_lanes(value)

        sums = [None] * 4
        for side, inside in ((0, space > 0), (1, space < S - 1)):
            keep = jnp.where(inside, 1.0, 0.0)
            got, mine = sides[side]
            near, far, mob = keep * got[0], keep * got[1], got[2]
            own, own_mob = mine[0], mine[2]
            beyond = keep * fine_rule(near, far + own + beside(near), mob)
            added = DIFFUSE * near
            before = outer[side]
            after = before + added
            grown = after * (1.0 - after * after) - before * (1.0 - before * before)
            first = added + DIFFUSE * (beyond + beside(added) - 6.0 * added)
            first = flagged * (first + REACTION * own_mob * grown)
            second = flagged * DIFFUSE * added
            change[side, 0] = first
            change[side, 1] = second
            sums[side] = near + far
            sums[2 + side] = first + second
        halved = halve_lanes(jnp.concatenate(sums, axis=0))
        for side in range(2):
            coarse_side = (0.5 * DIFFUSE * 0.25) * halved[side * Z : (side + 1) * Z]
            fine_side = 0.25 * halved[(2 + side) * Z : (3 + side) * Z]
            old_change[side] = coarse_side
            for tile, value in enumerate(edge_windows(fine_side - weight * coarse_side)):
                added_rows[side, tile] = value
        row = iota((CX, 128), 0)
        for tile in range(T):
            for z in range(HALF):
                low = added_rows[0, tile, pl.ds(z, 1), :]
                high = added_rows[1, tile, pl.ds(z, 1), :]
                change_here = jnp.where(row == 0, low, jnp.where(row == CX - 1, high, 0.0))
                sent[tile, z] = sent_in[tile, z] + change_here

    pl.when(space % 2 == 0)(lambda: run((odd, own_odd), (even, own_even)))
    pl.when(space % 2 == 1)(lambda: run((even, own_even), (odd, own_odd)))


def repair_body(fine_in, change, old_in, old_change, fine, coarse_old):
    row = iota((8, Y), 0)
    coarse_row = iota((CX, CY), 0)
    for z in range(Z):
        for side in range(2):
            here = pl.ds(z * X + side * 8, 8)
            first = change[side, 0, pl.ds(z, 1), :]
            second = change[side, 1, pl.ds(z, 1), :]
            last = 7 * side
            added = jnp.where(row == last, first, jnp.where(row == abs(last - 1), second, 0.0))
            fine[here, :] = fine_in[here, :] + added
        here = pl.ds(z * CX, CX)
        low, high = old_change[0, pl.ds(z, 1), :], old_change[1, pl.ds(z, 1), :]
        added = jnp.where(coarse_row == 0, low, jnp.where(coarse_row == CX - 1, high, 0.0))
        coarse_old[here, :] = old_in[here, :] + added


def pack_chain_body(terms, mob_tile, odd, even, late_odd, late_even):
    space = lax.axis_index("space")
    row = iota((HALF, CX, 128), 1)

    def of(number):
        return mob_tile[...] if number == MOBILITY else terms[number]

    def put(low, high, late_low, late_high):
        for pairs, first, last in ((EARLY, low, high), (LATE, late_low, late_high)):
            for k, ((one, rows), (other, rest)) in enumerate(pairs):
                here, there = of(one), of(other)
                place = pl.ds(k * HALF, HALF)
                first[place] = jnp.where(row < rows, here, pltpu.roll(there, rows, 1))
                last[place] = jnp.where(row >= rest, here, pltpu.roll(there, rest, 1))
        for k in range(2):
            for z in range(HALF):
                low[EARLY_TILES - 2 + k, pl.ds(z, 1), :] = mob_tile[z, pl.ds(4 + k, 1), :]
                high[EARLY_TILES - 2 + k, pl.ds(z, 1), :] = mob_tile[z, pl.ds(2 + k, 1), :]
        place = pl.ds(len(LATE) * HALF, HALF)
        late_low[place] = jnp.where(row < 4, terms[LAST], mob_tile[...])
        late_high[place] = jnp.where(row >= 4, terms[LAST], mob_tile[...])

    pl.when(space % 2 == 0)(lambda: put(odd, even, late_odd, late_even))
    pl.when(space % 2 == 1)(lambda: put(even, odd, late_even, late_odd))


def chain_parts(terms, shipments):
    place = {}
    for pairs, low, high in shipments:
        for k, ((one, rows), (other, rest)) in enumerate(pairs):
            place[one] = (low, high, k, 0, 0)
            place[other] = (low, high, k, CX - rest, CX - rows)

    def extended(number):
        own = terms[number]
        if number not in place:
            return jnp.concatenate([jnp.zeros_like(own), own, jnp.zeros_like(own)], axis=1)
        low, high, k, up, down = place[number]
        below, above = low[pl.ds(k * HALF, HALF)], high[pl.ds(k * HALF, HALF)]
        if up:
            below = pltpu.roll(below, up, 1)
            above = pltpu.roll(above, down, 1)
        return jnp.concatenate([below, own, above], axis=1)

    return extended


def inner_mobility(low, high):
    place = pl.ds((len(EARLY) - 1) * HALF, HALF)
    return pltpu.roll(low[place], 4, 1), pltpu.roll(high[place], 4, 1)


def early_mobility(low, high):
    below, above = inner_mobility(low, high)
    row = iota((CX, 128), 0)
    lows, highs = [], []
    for z in range(HALF):
        low_rows = [low[EARLY_TILES - 2 + k, pl.ds(z, 1), :] for k in range(2)]
        high_rows = [high[EARLY_TILES - 2 + k, pl.ds(z, 1), :] for k in range(2)]
        outer = jnp.where(row == 2, low_rows[0], jnp.where(row == 3, low_rows[1], 0.0))
        lows.append(jnp.where(row >= 4, below[z], outer)[None])
        outer = jnp.where(row == 4, high_rows[0], jnp.where(row == 5, high_rows[1], 0.0))
        highs.append(jnp.where(row < 4, above[z], outer)[None])
    return jnp.concatenate(lows, axis=0), jnp.concatenate(highs, axis=0)


def late_mobility(low, high, late_low, late_high):
    below, above = inner_mobility(low, high)
    place = pl.ds(len(LATE) * HALF, HALF)
    row = iota((HALF, CX, 128), 1)
    return (
        jnp.where(row >= 4, below, late_low[place]),
        jnp.where(row < 4, above, late_high[place]),
    )


def around_chain(space, turn):
    row = iota((1, SPAN, 128), 1) - CX + space * CX
    column = iota((1, SPAN, 128), 2) % 64 - MARGIN + turn * OWN
    inside = (row >= 0) & (row < S * CX) & (column >= 0) & (column < CY)
    return jnp.where(inside, 0.5 * DIFFUSE, 0.0)


def chain_step(state, rate, weight):
    lane = iota((1, SPAN, 128), 2)
    crossed_up = jnp.where(lane < 64, pltpu.roll(state[:1], 64, 2), 0.0)
    crossed_down = jnp.where(lane >= 64, pltpu.roll(state[HALF - 1 :], 64, 2), 0.0)
    stacked = jnp.concatenate([state[1:], crossed_up], axis=0)
    stacked += jnp.concatenate([crossed_down, state[:-1]], axis=0)
    beside = pltpu.roll(state, 1, 1) + pltpu.roll(state, SPAN - 1, 1)
    beside += pltpu.roll(state, 1, 2) + pltpu.roll(state, 127, 2)
    return coarse_rule(state, weight * beside, stacked, rate)


def returned(advanced):
    own = advanced[:, CX : 2 * CX, :]
    lane = iota((4, CX, 128), 2)
    return jnp.where(
        lane % 64 < OWN,
        pltpu.roll(own[:4], 128 - MARGIN, 2),
        pltpu.roll(own[4:], OWN - MARGIN, 2),
    )


def run_chain(state, extended, rate, weight, numbers, back):
    for number in numbers:
        kept, given = chain_step(state, rate, weight)
        back[number] = returned(kept + given)
        if number < T - 1:
            state = kept + (given + extended(number))
    return state


class Beside:
    def __init__(self, ref, inside):
        self.ref, self.keep = ref, jnp.where(inside, 1.0, 0.0)

    def __getitem__(self, index):
        return self.keep * self.ref[index]


def sorted_by_side(run, *pairs):
    space = lax.axis_index("space")

    def call_with(first):
        sides = []
        for pair in pairs:
            low, high = pair[first], pair[1 - first]
            sides.append((Beside(low, space > 0), Beside(high, space < S - 1)))
        run(*sides)

    pl.when(space % 2 == 0)(lambda: call_with(0))
    pl.when(space % 2 == 1)(lambda: call_with(1))


def chain_rate(below, mob_tile, above):
    return (2.0 * REACTION) * jnp.concatenate([below, mob_tile[...], above], axis=1)


def chain_one_body(terms, mob_tile, odd, even, back, middle):
    weight = around_chain(lax.axis_index("space"), lax.axis_index("tm"))
    back[0] = jnp.zeros((4, CX, 128), jnp.float32)

    def run(early):
        extended = chain_parts(terms, [(EARLY, *early)])
        below, above = early_mobility(*early)
        rate = chain_rate(below, mob_tile, above)
        state = run_chain(extended(0), extended, rate, weight, range(1, FIRST + 1), back)
        middle[...] = state[:, CX : 2 * CX, :]

    sorted_by_side(run, (odd, even))


def chain_two_body(
    terms, mob_tile, odd, even, late_odd, late_even, first, middle, mid_odd, mid_even, back
):
    weight = around_chain(lax.axis_index("space"), lax.axis_index("tm"))
    back[pl.ds(0, FIRST + 1)] = first[...]
    late_pairs = LATE + (((LAST, 4), (MOBILITY, 4)),)

    def run(early, late, ends):
        extended = chain_parts(terms, [(EARLY, *early), (late_pairs, *late)])
        mob_below, mob_above = late_mobility(*early, *late)
        rate = chain_rate(mob_below, mob_tile, mob_above)
        state = jnp.concatenate([ends[0][...], middle[...], ends[1][...]], axis=1)
        run_chain(state, extended, rate, weight, range(FIRST + 1, T), back)

    sorted_by_side(run, (odd, even), (late_odd, late_even), (mid_odd, mid_even))


def finish_body(fine, coarse_old, arrived, out_far, parts, out, done):
    turn = lax.axis_index("tm")
    lane = iota((CX, 128), 1)
    weight = jnp.where(turn > 0, 1.0, 0.0)
    pick = (iota((256, 256), 0) % 128 == iota((256, 256), 1) // 2).astype(jnp.bfloat16)
    stores = []
    deep = Z // 4
    few, many = deep * CX, deep * X
    chunks = CY // 128
    for group in range(4):
        for part in range(chunks):
            planes = []
            for quarter in range(4):
                total = None
                for k in range(4):
                    block = arrived[4 * part + k, quarter]
                    shift = (OWN * (k - group)) % 128
                    block = pltpu.roll(block, shift, 1) if shift else block
                    total = block if total is None else jnp.where(lane >= OWN * k, block, total)
                planes.append(total)
            advanced = jnp.concatenate(planes, axis=0)
            old = coarse_old[pl.ds(group * few, few), pl.ds(128 * part, 128)]
            both = jnp.concatenate(split(weight * (advanced - old)), axis=1)
            wide = jnp.dot(both, pick, preferred_element_type=jnp.float32)
            for half in range(2):
                block = wide[:, 128 * half : 128 * (half + 1)]
                start = (2 * part + half) * many
                parts[group, pl.ds(start, few, stride=2), :] = block
                parts[group, pl.ds(start + 1, few, stride=2), :] = block
        rows = pl.ds(group * many, many)
        for part in range(2 * chunks):
            columns = pl.ds(128 * part, 128)
            out[rows, columns] = fine[rows, columns] + parts[group, pl.ds(part * many, many), :]
        stores.append(
            pltpu.make_async_copy(out.at[rows, :], out_far.at[rows, :], done.at[group])
        )
        stores[-1].start()
    for store in stores:
        store.wait()


def pack_fine(iterate, mobility):
    rows = jax.ShapeDtypeStruct((3, Z, Y), jnp.float32)
    return pl.pallas_call(
        pack_fine_body,
        out_shape=[rows, rows],
        in_specs=[pl.BlockSpec(memory_space=pltpu.HBM)] * 2,
        out_specs=[pl.BlockSpec(memory_space=pltpu.VMEM)] * 2,
        scratch_shapes=[pltpu.SemaphoreType.DMA((6,))],
        compiler_params=pltpu.CompilerParams(vmem_limit_bytes=PACK_VMEM),
        cost_estimate=pl.CostEstimate(flops=0, bytes_accessed=400_000, transcendentals=0),
    )(iterate, mobility)


def finish(fine, coarse_old, arrived):
    return pl.pallas_call(
        finish_body,
        out_shape=jax.ShapeDtypeStruct((ROWS, Y), jnp.float32),
        in_specs=[pl.BlockSpec(memory_space=pltpu.VMEM)] * 3,
        out_specs=pl.BlockSpec(memory_space=pltpu.HBM),
        scratch_shapes=[
            pltpu.VMEM((4, Y // 128 * X * Z // 4, 128), jnp.float32),
            pltpu.VMEM((ROWS, Y), jnp.float32),
            pltpu.SemaphoreType.DMA((4,)),
        ],
        compiler_params=pltpu.CompilerParams(vmem_limit_bytes=VMEM_LIMIT),
        cost_estimate=pl.CostEstimate(flops=0, bytes_accessed=4_000_000, transcendentals=0),
    )(fine, coarse_old, arrived)


def exchange(odd, even):
    route = []
    for turn in range(T):
        for space in range(S):
            if space in (0, S - 1):
                target = (turn ^ 1) * S + space
            else:
                target = turn * S + space + 2 * (space % 2) - 1
            route.append((turn * S + space, target))
    even_route = [(i, i + 1 - 2 * (i % 2)) for i in range(S)]
    return lax.ppermute(odd, ("tm", "space"), route), lax.ppermute(even, "space", even_route)


def local(iterate, fine_prev, mobility, pending):
    tile = (HALF, CX, 128)
    early = (EARLY_TILES, CX, 128)
    late = (LATE_TILES, CX, 128)
    fields = [field.reshape(ROWS, Y) for field in (iterate, mobility, fine_prev)]
    own_odd, own_even = pack_fine(iterate[0], mobility)
    odd, even = exchange(own_odd, own_even)
    stepped, old_part, mob_tile, outer, flag = call(
        before_body, [(ROWS, Y), (CROWS, CY), tile, (2, Z, Y), (8, 128)], [(Y // 256, ROWS, 128)]
    )(pending.reshape(1, T), fields[0], fields[1])
    fine_part, sent = call(second_body, [(ROWS, Y), (T,) + tile], [(Y // 256, ROWS, 128)])(
        flag, stepped, fields[1], old_part, fields[2]
    )
    sent, change, old_change = call(
        edge_body,
        [(T,) + tile, (2, 2, Z, Y), (2, Z, CY)],
        [(2, T, HALF, 128)],
    )(flag, own_odd, own_even, odd, even, outer, sent)
    terms = lax.all_to_all(sent, "tm", 0, 0)
    odd, even, late_odd, late_even = call(pack_chain_body, [early, early, late, late])(
        terms, mob_tile
    )
    odd, even = exchange(odd, even)
    late_odd, late_even = exchange(late_odd, late_even)
    fine, coarse_old = call(repair_body, [(ROWS, Y), (CROWS, CY)])(
        fine_part, change, old_part, old_change
    )
    odd, even, fine, coarse_old = lax.optimization_barrier((odd, even, fine, coarse_old))
    part = (4, CX, 128)
    first, middle = call(chain_one_body, [(FIRST + 1,) + part, tile])(
        terms, mob_tile, odd, even
    )
    mid_odd, mid_even = exchange(middle, middle)
    (back,) = call(chain_two_body, [(T,) + part])(
        terms, mob_tile, odd, even, late_odd, late_even, first, middle, mid_odd, mid_even
    )
    arrived = lax.all_to_all(back, "tm", 0, 0)
    return finish(fine, coarse_old, arrived).reshape(1, Z, X, Y)


def solution(mesh):
    placed = (
        P("tm", None, "space", None),
        P("tm", None, "space", None),
        P(None, "space", None),
        P(),
    )
    return jax.shard_map(
        local, mesh=mesh, in_specs=placed, out_specs=P("tm", None, "space", None), check_vma=False
    )
```

```python
import jax
import jax.numpy as jnp
from jax import lax
from jax.experimental import pallas as pl
from jax.experimental.pallas import tpu as pltpu
from jax.sharding import PartitionSpec as P

Z = 16
X = 16
Y = 1024
T = 16
S = 16
CX = X // 2
CY = Y // 2
ROWS = Z * X
CROWS = Z * CX
OWN = CY // T
MARGIN = 16
HALF = Z // 2
FIRST = 7
SPAN = 3 * CX

DIFFUSE = 0.15
REACTION = 0.1
VMEM_LIMIT = 48 * 1024 * 1024
PACK_VMEM = 54272 * 1024


MOBILITY = T
EARLY = (
    ((0, 7), (6, 1)),
    ((1, 6), (5, 2)),
    ((2, 5), (4, 3)),
    ((3, 4), (MOBILITY, 4)),
)
LATE = (
    ((8, 7), (14, 1)),
    ((9, 6), (13, 2)),
    ((10, 5), (12, 3)),
)
LAST = 11
EARLY_TILES = len(EARLY) * HALF + 2
LATE_TILES = (len(LATE) + 1) * HALF


def call(body, outs, scratch=(), flops=0):
    return pl.pallas_call(
        body,
        out_shape=[jax.ShapeDtypeStruct(shape, jnp.float32) for shape in outs],
        scratch_shapes=[pltpu.VMEM(shape, jnp.float32) for shape in scratch],
        compiler_params=pltpu.CompilerParams(vmem_limit_bytes=VMEM_LIMIT),
        cost_estimate=pl.CostEstimate(flops=flops, bytes_accessed=4_000_000, transcendentals=0),
    )


def iota(shape, axis):
    return lax.broadcasted_iota(jnp.int32, shape, axis)


def split(value):
    high = value.astype(jnp.bfloat16)
    low = (value - high.astype(jnp.float32)).astype(jnp.bfloat16)
    return high, low


def restrict(value, parts):
    high, low = split(value)
    pick = (iota((256, 128), 0) // 2 == iota((256, 128), 1)).astype(jnp.bfloat16)
    for k in range(Y // 256):
        chunk = slice(256 * k, 256 * (k + 1))
        parts[k] = jnp.dot(high[:, chunk], pick, preferred_element_type=jnp.float32) + jnp.dot(
            low[:, chunk], pick, preferred_element_type=jnp.float32
        )
    pieces = [
        parts[k, pl.ds(0, CROWS, stride=2), :] + parts[k, pl.ds(1, CROWS, stride=2), :]
        for k in range(Y // 256)
    ]
    return 0.25 * jnp.concatenate(pieces, axis=1)


def halve_lanes(value):
    high, low = split(value)
    pick = (iota((256, 128), 0) // 2 == iota((256, 128), 1)).astype(jnp.bfloat16)
    pieces = []
    for k in range(Y // 256):
        chunk = slice(256 * k, 256 * (k + 1))
        pieces.append(
            jnp.dot(high[:, chunk], pick, preferred_element_type=jnp.float32)
            + jnp.dot(low[:, chunk], pick, preferred_element_type=jnp.float32)
        )
    return jnp.concatenate(pieces, axis=1)


def beside_lanes(value):
    count = value.shape[-1]
    axis = value.ndim - 1
    before = pltpu.roll(value, 1, axis)
    after = pltpu.roll(value, count - 1, axis)
    lane = iota(value.shape[:-1] + (128,), axis)
    before = jnp.concatenate(
        [jnp.where(lane == 0, 0.0, before[..., :128]), before[..., 128:]], axis=axis
    )
    after = jnp.concatenate(
        [after[..., :-128], jnp.where(lane == 127, 0.0, after[..., -128:])], axis=axis
    )
    return before + after


def fine_rule(center, around, mobility):
    return DIFFUSE * around + REACTION * (center * (1.0 + mobility * (1.0 - center * center)))


def fine_tile(ref, mob_ref, z, tile, low_row, high_row):
    base = z * X + tile * 8
    center = ref[pl.ds(base, 8), :]
    row = iota((8, Y), 0)
    below = ref[pl.ds(base - 1, 1), :] if tile else low_row
    above = high_row if tile else ref[pl.ds(base + 8, 1), :]
    around = jnp.where(row == 0, below, pltpu.roll(center, 1, 0))
    around += jnp.where(row == 7, above, pltpu.roll(center, 7, 0))
    around += beside_lanes(center)
    if z > 0:
        around += ref[pl.ds(base - X, 8), :]
    if z < Z - 1:
        around += ref[pl.ds(base + X, 8), :]
    return fine_rule(center, around, mob_ref[pl.ds(base, 8), :])


def pack_fine_body(iterate, mobility, odd, even, done):
    space = lax.axis_index("space")

    def put(low, high):
        moves = []
        for out, near, far in ((low, 0, 1), (high, X - 1, X - 2)):
            for k, (source, inner) in enumerate(((iterate, near), (iterate, far), (mobility, near))):
                moves.append(
                    pltpu.make_async_copy(source.at[:, inner, :], out.at[k], done.at[len(moves)])
                )
        for move in moves:
            move.start()
        for move in moves:
            move.wait()

    pl.when(space % 2 == 0)(lambda: put(odd, even))
    pl.when(space % 2 == 1)(lambda: put(even, odd))


def windows(value):
    count = CY // 128
    blank = jnp.zeros((HALF, CX, 128), jnp.float32)
    lane = iota((HALF, CX, 128), 2)
    moved = {}

    def piece(half, index, amount):
        if not 0 <= index < count:
            return blank
        if (half, index, amount) not in moved:
            planes = value[HALF * half : HALF * (half + 1)]
            moved[half, index, amount] = pltpu.roll(
                planes[:, :, 128 * index : 128 * (index + 1)], amount, 2
            )
        return moved[half, index, amount]

    tiles = []
    for tile in range(T):
        start = tile * OWN - MARGIN
        first = start // 128
        offset = start - first * 128
        parts = []
        for half in range(2):
            amount = (64 * half - offset) % 128
            part = piece(half, first, amount)
            if offset + 64 > 128:
                after = piece(half, first + 1, amount)
                part = jnp.where(lane < 64 * half + 128 - offset, part, after)
            parts.append(part)
        tiles.append(jnp.where(lane < 64, parts[0], parts[1]))
    return tiles


def turned(value, tile):
    start = tile * OWN - MARGIN
    wide = jnp.concatenate([value, jnp.zeros((Z, CX, 128), jnp.float32)], axis=2)
    count = CY + 128
    first = pltpu.roll(wide[:HALF], (count - start) % count, 2)[:, :, :128]
    second = pltpu.roll(wide[HALF:], (count - start + 64) % count, 2)[:, :, :128]
    return jnp.where(iota((HALF, CX, 128), 2) < 64, first, second)


def partial_step(source, mobility, target):
    none = jnp.zeros((1, Y), jnp.float32)
    for z in range(Z):
        for tile in range(X // 8):
            target[pl.ds(z * X + tile * 8, 8), :] = fine_tile(
                source, mobility, z, tile, none, none
            )


def before_body(pending, iterate, mobility, stepped, coarse_old, mob_tile, outer, flag, parts):
    turn = lax.axis_index("tm")
    mine = jnp.where(iota((1, T), 1) == turn, pending[...], 0)
    chosen = jnp.sum(mine, axis=1, keepdims=True)
    flag[...] = jnp.broadcast_to(jnp.where(chosen > 0, 1.0, 0.0), (8, 128))
    partial_step(iterate, mobility, stepped)
    for side, inner in ((0, 0), (1, X - 1)):
        for z in range(Z):
            outer[side, pl.ds(z, 1), :] = stepped[pl.ds(z * X + inner, 1), :]
    coarse_mobility = restrict(mobility[...], parts).reshape(Z, CX, CY)
    start = restrict(iterate[...], parts).reshape(Z, CX, CY)
    row = iota((Z, CX, CY), 1)
    around = jnp.where(row == 0, 0.0, pltpu.roll(start, 1, 1))
    around += jnp.where(row == CX - 1, 0.0, pltpu.roll(start, CX - 1, 1))
    around += beside_lanes(start)
    flat = jnp.zeros((1, CX, CY), jnp.float32)
    stacked = jnp.concatenate([start[1:], flat], axis=0)
    stacked += jnp.concatenate([flat, start[:-1]], axis=0)
    rate = 2.0 * REACTION * coarse_mobility
    kept, given = coarse_rule(start, 0.5 * DIFFUSE * around, stacked, rate)
    coarse_old[...] = (kept + given).reshape(CROWS, CY)
    mob_tile[...] = turned(coarse_mobility, turn)


def second_body(flag, stepped, mobility, coarse_old, previous, fine, sent, parts):
    turn = lax.axis_index("tm")
    flagged = jnp.max(flag[...]) > 0.5
    pl.when(flagged)(lambda: partial_step(stepped, mobility, fine))

    @pl.when(jnp.logical_not(flagged))
    def _():
        fine[...] = previous[...]

    weight = jnp.where(turn > 0, 1.0, 0.0)
    term = restrict(fine[...], parts) - weight * coarse_old[...]
    for tile, value in enumerate(windows(term.reshape(Z, CX, CY))):
        sent[tile] = value


def coarse_rule(center, beside, stacked, rate):
    bottom = 1.0 + rate * (center * center)
    inverse = pltpu.reciprocal(bottom, approx=True)
    inverse = inverse * (2.0 - bottom * inverse)
    kept = center * ((1.0 + rate) * inverse - 6.0 * DIFFUSE)
    return kept, beside + 2.0 * DIFFUSE * stacked


def edge_windows(value):
    count = CY // 128
    lane = iota((HALF, 128), 1)
    moved = {}

    def piece(half, index, amount):
        if not 0 <= index < count:
            return jnp.zeros((HALF, 128), jnp.float32)
        if (half, index, amount) not in moved:
            part = value[HALF * half : HALF * (half + 1), 128 * index : 128 * (index + 1)]
            moved[half, index, amount] = pltpu.roll(part, amount, 1)
        return moved[half, index, amount]

    tiles = []
    for tile in range(T):
        start = tile * OWN - MARGIN
        first = start // 128
        offset = start - first * 128
        parts = []
        for half in range(2):
            amount = (64 * half - offset) % 128
            part = piece(half, first, amount)
            if offset + 64 > 128:
                after = piece(half, first + 1, amount)
                part = jnp.where(lane < 64 * half + 128 - offset, part, after)
            parts.append(part)
        tiles.append(jnp.where(lane < 64, parts[0], parts[1]))
    return tiles


def edge_body(
    flag, own_odd, own_even, even, odd, outer, sent_in, sent, change, old_change, added_rows
):
    space = lax.axis_index("space")
    turn = lax.axis_index("tm")

    def run(*sides):
        flagged = flag[pl.ds(0, 1), pl.ds(0, 1)]
        weight = jnp.where(turn > 0, 1.0, 0.0)
        plane = iota((Z, Y), 0)

        def beside(value):
            total = jnp.where(plane == 0, 0.0, pltpu.roll(value, 1, 0))
            total += jnp.where(plane == Z - 1, 0.0, pltpu.roll(value, Z - 1, 0))
            return total + beside_lanes(value)

        sums = [None] * 4
        for side, inside in ((0, space > 0), (1, space < S - 1)):
            keep = jnp.where(inside, 1.0, 0.0)
            got, mine = sides[side]
            near, far, mob = keep * got[0], keep * got[1], got[2]
            own, own_mob = mine[0], mine[2]
            beyond = keep * fine_rule(near, far + own + beside(near), mob)
            added = DIFFUSE * near
            before = outer[side]
            after = before + added
            grown = after * (1.0 - after * after) - before * (1.0 - before * before)
            first = added + DIFFUSE * (beyond + beside(added) - 6.0 * added)
            first = flagged * (first + REACTION * own_mob * grown)
            second = flagged * DIFFUSE * added
            change[side, 0] = first
            change[side, 1] = second
            sums[side] = near + far
            sums[2 + side] = first + second
        halved = halve_lanes(jnp.concatenate(sums, axis=0))
        for side in range(2):
            coarse_side = (0.5 * DIFFUSE * 0.25) * halved[side * Z : (side + 1) * Z]
            fine_side = 0.25 * halved[(2 + side) * Z : (3 + side) * Z]
            old_change[side] = coarse_side
            for tile, value in enumerate(edge_windows(fine_side - weight * coarse_side)):
                added_rows[side, tile] = value
        row = iota((CX, 128), 0)
        for tile in range(T):
            for z in range(HALF):
                low = added_rows[0, tile, pl.ds(z, 1), :]
                high = added_rows[1, tile, pl.ds(z, 1), :]
                change_here = jnp.where(row == 0, low, jnp.where(row == CX - 1, high, 0.0))
                sent[tile, z] = sent_in[tile, z] + change_here

    pl.when(space % 2 == 0)(lambda: run((odd, own_odd), (even, own_even)))
    pl.when(space % 2 == 1)(lambda: run((even, own_even), (odd, own_odd)))


def repair_body(fine_in, change, old_in, old_change, fine, coarse_old):
    row = iota((8, Y), 0)
    coarse_row = iota((CX, CY), 0)
    for z in range(Z):
        for side in range(2):
            here = pl.ds(z * X + side * 8, 8)
            first = change[side, 0, pl.ds(z, 1), :]
            second = change[side, 1, pl.ds(z, 1), :]
            last = 7 * side
            added = jnp.where(row == last, first, jnp.where(row == abs(last - 1), second, 0.0))
            fine[here, :] = fine_in[here, :] + added
        here = pl.ds(z * CX, CX)
        low, high = old_change[0, pl.ds(z, 1), :], old_change[1, pl.ds(z, 1), :]
        added = jnp.where(coarse_row == 0, low, jnp.where(coarse_row == CX - 1, high, 0.0))
        coarse_old[here, :] = old_in[here, :] + added


def pack_chain_body(terms, mob_tile, odd, even, late_odd, late_even):
    space = lax.axis_index("space")
    row = iota((HALF, CX, 128), 1)

    def of(number):
        return mob_tile[...] if number == MOBILITY else terms[number]

    def put(low, high, late_low, late_high):
        for pairs, first, last in ((EARLY, low, high), (LATE, late_low, late_high)):
            for k, ((one, rows), (other, rest)) in enumerate(pairs):
                here, there = of(one), of(other)
                place = pl.ds(k * HALF, HALF)
                first[place] = jnp.where(row < rows, here, pltpu.roll(there, rows, 1))
                last[place] = jnp.where(row >= rest, here, pltpu.roll(there, rest, 1))
        for k in range(2):
            for z in range(HALF):
                low[EARLY_TILES - 2 + k, pl.ds(z, 1), :] = mob_tile[z, pl.ds(4 + k, 1), :]
                high[EARLY_TILES - 2 + k, pl.ds(z, 1), :] = mob_tile[z, pl.ds(2 + k, 1), :]
        place = pl.ds(len(LATE) * HALF, HALF)
        late_low[place] = jnp.where(row < 4, terms[LAST], mob_tile[...])
        late_high[place] = jnp.where(row >= 4, terms[LAST], mob_tile[...])

    pl.when(space % 2 == 0)(lambda: put(odd, even, late_odd, late_even))
    pl.when(space % 2 == 1)(lambda: put(even, odd, late_even, late_odd))


def chain_parts(terms, shipments):
    place = {}
    for pairs, low, high in shipments:
        for k, ((one, rows), (other, rest)) in enumerate(pairs):
            place[one] = (low, high, k, 0, 0)
            place[other] = (low, high, k, CX - rest, CX - rows)

    def extended(number):
        own = terms[number]
        if number not in place:
            return jnp.concatenate([jnp.zeros_like(own), own, jnp.zeros_like(own)], axis=1)
        low, high, k, up, down = place[number]
        below, above = low[pl.ds(k * HALF, HALF)], high[pl.ds(k * HALF, HALF)]
        if up:
            below = pltpu.roll(below, up, 1)
            above = pltpu.roll(above, down, 1)
        return jnp.concatenate([below, own, above], axis=1)

    return extended


def inner_mobility(low, high):
    place = pl.ds((len(EARLY) - 1) * HALF, HALF)
    return pltpu.roll(low[place], 4, 1), pltpu.roll(high[place], 4, 1)


def early_mobility(low, high):
    below, above = inner_mobility(low, high)
    row = iota((CX, 128), 0)
    lows, highs = [], []
    for z in range(HALF):
        low_rows = [low[EARLY_TILES - 2 + k, pl.ds(z, 1), :] for k in range(2)]
        high_rows = [high[EARLY_TILES - 2 + k, pl.ds(z, 1), :] for k in range(2)]
        outer = jnp.where(row == 2, low_rows[0], jnp.where(row == 3, low_rows[1], 0.0))
        lows.append(jnp.where(row >= 4, below[z], outer)[None])
        outer = jnp.where(row == 4, high_rows[0], jnp.where(row == 5, high_rows[1], 0.0))
        highs.append(jnp.where(row < 4, above[z], outer)[None])
    return jnp.concatenate(lows, axis=0), jnp.concatenate(highs, axis=0)


def late_mobility(low, high, late_low, late_high):
    below, above = inner_mobility(low, high)
    place = pl.ds(len(LATE) * HALF, HALF)
    row = iota((HALF, CX, 128), 1)
    return (
        jnp.where(row >= 4, below, late_low[place]),
        jnp.where(row < 4, above, late_high[place]),
    )


def around_chain(space, turn):
    row = iota((1, SPAN, 128), 1) - CX + space * CX
    column = iota((1, SPAN, 128), 2) % 64 - MARGIN + turn * OWN
    inside = (row >= 0) & (row < S * CX) & (column >= 0) & (column < CY)
    return jnp.where(inside, 0.5 * DIFFUSE, 0.0)


def chain_step(state, rate, weight):
    lane = iota((1, SPAN, 128), 2)
    crossed_up = jnp.where(lane < 64, pltpu.roll(state[:1], 64, 2), 0.0)
    crossed_down = jnp.where(lane >= 64, pltpu.roll(state[HALF - 1 :], 64, 2), 0.0)
    stacked = jnp.concatenate([state[1:], crossed_up], axis=0)
    stacked += jnp.concatenate([crossed_down, state[:-1]], axis=0)
    beside = pltpu.roll(state, 1, 1) + pltpu.roll(state, SPAN - 1, 1)
    beside += pltpu.roll(state, 1, 2) + pltpu.roll(state, 127, 2)
    return coarse_rule(state, weight * beside, stacked, rate)


def returned(advanced):
    own = advanced[:, CX : 2 * CX, :]
    lane = iota((4, CX, 128), 2)
    return jnp.where(
        lane % 64 < OWN,
        pltpu.roll(own[:4], 128 - MARGIN, 2),
        pltpu.roll(own[4:], OWN - MARGIN, 2),
    )


def run_chain(state, extended, rate, weight, numbers, back):
    for number in numbers:
        kept, given = chain_step(state, rate, weight)
        back[number] = returned(kept + given)
        if number < T - 1:
            state = kept + (given + extended(number))
    return state


class Beside:
    def __init__(self, ref, inside):
        self.ref, self.keep = ref, jnp.where(inside, 1.0, 0.0)

    def __getitem__(self, index):
        return self.keep * self.ref[index]


def sorted_by_side(run, *pairs):
    space = lax.axis_index("space")

    def call_with(first):
        sides = []
        for pair in pairs:
            low, high = pair[first], pair[1 - first]
            sides.append((Beside(low, space > 0), Beside(high, space < S - 1)))
        run(*sides)

    pl.when(space % 2 == 0)(lambda: call_with(0))
    pl.when(space % 2 == 1)(lambda: call_with(1))


def chain_rate(below, mob_tile, above):
    return (2.0 * REACTION) * jnp.concatenate([below, mob_tile[...], above], axis=1)


def chain_one_body(terms, mob_tile, odd, even, back, middle):
    weight = around_chain(lax.axis_index("space"), lax.axis_index("tm"))
    back[0] = jnp.zeros((4, CX, 128), jnp.float32)

    def run(early):
        extended = chain_parts(terms, [(EARLY, *early)])
        below, above = early_mobility(*early)
        rate = chain_rate(below, mob_tile, above)
        state = run_chain(extended(0), extended, rate, weight, range(1, FIRST + 1), back)
        middle[...] = state[:, CX : 2 * CX, :]

    sorted_by_side(run, (odd, even))


def chain_two_body(
    terms, mob_tile, odd, even, late_odd, late_even, first, middle, mid_odd, mid_even, back
):
    weight = around_chain(lax.axis_index("space"), lax.axis_index("tm"))
    back[pl.ds(0, FIRST + 1)] = first[...]
    late_pairs = LATE + (((LAST, 4), (MOBILITY, 4)),)

    def run(early, late, ends):
        extended = chain_parts(terms, [(EARLY, *early), (late_pairs, *late)])
        mob_below, mob_above = late_mobility(*early, *late)
        rate = chain_rate(mob_below, mob_tile, mob_above)
        state = jnp.concatenate([ends[0][...], middle[...], ends[1][...]], axis=1)
        run_chain(state, extended, rate, weight, range(FIRST + 1, T), back)

    sorted_by_side(run, (odd, even), (late_odd, late_even), (mid_odd, mid_even))


def finish_body(fine, coarse_old, arrived, out_far, parts, out, done):
    turn = lax.axis_index("tm")
    lane = iota((CX, 128), 1)
    weight = jnp.where(turn > 0, 1.0, 0.0)
    pick = (iota((256, 256), 0) % 128 == iota((256, 256), 1) // 2).astype(jnp.bfloat16)
    stores = []
    deep = Z // 4
    few, many = deep * CX, deep * X
    chunks = CY // 128
    for group in range(4):
        for part in range(chunks):
            planes = []
            for quarter in range(4):
                total = None
                for k in range(4):
                    block = arrived[4 * part + k, quarter]
                    shift = (OWN * (k - group)) % 128
                    block = pltpu.roll(block, shift, 1) if shift else block
                    total = block if total is None else jnp.where(lane >= OWN * k, block, total)
                planes.append(total)
            advanced = jnp.concatenate(planes, axis=0)
            old = coarse_old[pl.ds(group * few, few), pl.ds(128 * part, 128)]
            both = jnp.concatenate(split(weight * (advanced - old)), axis=1)
            wide = jnp.dot(both, pick, preferred_element_type=jnp.float32)
            for half in range(2):
                block = wide[:, 128 * half : 128 * (half + 1)]
                start = (2 * part + half) * many
                parts[group, pl.ds(start, few, stride=2), :] = block
                parts[group, pl.ds(start + 1, few, stride=2), :] = block
        rows = pl.ds(group * many, many)
        for part in range(2 * chunks):
            columns = pl.ds(128 * part, 128)
            out[rows, columns] = fine[rows, columns] + parts[group, pl.ds(part * many, many), :]
        stores.append(
            pltpu.make_async_copy(out.at[rows, :], out_far.at[rows, :], done.at[group])
        )
        stores[-1].start()
    for store in stores:
        store.wait()


def pack_fine(iterate, mobility):
    rows = jax.ShapeDtypeStruct((3, Z, Y), jnp.float32)
    return pl.pallas_call(
        pack_fine_body,
        out_shape=[rows, rows],
        in_specs=[pl.BlockSpec(memory_space=pltpu.HBM)] * 2,
        out_specs=[pl.BlockSpec(memory_space=pltpu.VMEM)] * 2,
        scratch_shapes=[pltpu.SemaphoreType.DMA((6,))],
        compiler_params=pltpu.CompilerParams(vmem_limit_bytes=PACK_VMEM),
        cost_estimate=pl.CostEstimate(flops=0, bytes_accessed=400_000, transcendentals=0),
    )(iterate, mobility)


def finish(fine, coarse_old, arrived):
    return pl.pallas_call(
        finish_body,
        out_shape=jax.ShapeDtypeStruct((ROWS, Y), jnp.float32),
        in_specs=[pl.BlockSpec(memory_space=pltpu.VMEM)] * 3,
        out_specs=pl.BlockSpec(memory_space=pltpu.HBM),
        scratch_shapes=[
            pltpu.VMEM((4, Y // 128 * X * Z // 4, 128), jnp.float32),
            pltpu.VMEM((ROWS, Y), jnp.float32),
            pltpu.SemaphoreType.DMA((4,)),
        ],
        compiler_params=pltpu.CompilerParams(vmem_limit_bytes=VMEM_LIMIT),
        cost_estimate=pl.CostEstimate(flops=0, bytes_accessed=4_000_000, transcendentals=0),
    )(fine, coarse_old, arrived)


def exchange(odd, even):
    route = []
    for turn in range(T):
        for space in range(S):
            if space in (0, S - 1):
                target = (turn ^ 1) * S + space
            else:
                target = turn * S + space + 2 * (space % 2) - 1
            route.append((turn * S + space, target))
    even_route = [(i, i + 1 - 2 * (i % 2)) for i in range(S)]
    return lax.ppermute(odd, ("tm", "space"), route), lax.ppermute(even, "space", even_route)


def local(iterate, fine_prev, mobility, pending):
    tile = (HALF, CX, 128)
    early = (EARLY_TILES, CX, 128)
    late = (LATE_TILES, CX, 128)
    fields = [field.reshape(ROWS, Y) for field in (iterate, mobility, fine_prev)]
    own_odd, own_even = pack_fine(iterate[0], mobility)
    odd, even = exchange(own_odd, own_even)
    stepped, old_part, mob_tile, outer, flag = call(
        before_body, [(ROWS, Y), (CROWS, CY), tile, (2, Z, Y), (8, 128)], [(Y // 256, ROWS, 128)]
    )(pending.reshape(1, T), fields[0], fields[1])
    fine_part, sent = call(second_body, [(ROWS, Y), (T,) + tile], [(Y // 256, ROWS, 128)])(
        flag, stepped, fields[1], old_part, fields[2]
    )
    sent, change, old_change = call(
        edge_body,
        [(T,) + tile, (2, 2, Z, Y), (2, Z, CY)],
        [(2, T, HALF, 128)],
    )(flag, own_odd, own_even, even, odd, outer, sent)
    terms = lax.all_to_all(sent, "tm", 0, 0)
    odd, even, late_odd, late_even = call(pack_chain_body, [early, early, late, late])(
        terms, mob_tile
    )
    odd, even = exchange(odd, even)
    late_odd, late_even = exchange(late_odd, late_even)
    fine, coarse_old = call(repair_body, [(ROWS, Y), (CROWS, CY)])(
        fine_part, change, old_part, old_change
    )
    odd, even, fine, coarse_old = lax.optimization_barrier((odd, even, fine, coarse_old))
    part = (4, CX, 128)
    first, middle = call(chain_one_body, [(FIRST + 1,) + part, tile])(
        terms, mob_tile, odd, even
    )
    mid_odd, mid_even = exchange(middle, middle)
    (back,) = call(chain_two_body, [(T,) + part])(
        terms, mob_tile, odd, even, late_odd, late_even, first, middle, mid_odd, mid_even
    )
    arrived = lax.all_to_all(back, "tm", 0, 0)
    return finish(fine, coarse_old, arrived).reshape(1, Z, X, Y)


def solution(mesh):
    placed = (
        P("tm", None, "space", None),
        P("tm", None, "space", None),
        P(None, "space", None),
        P(),
    )
    return jax.shard_map(
        local, mesh=mesh, in_specs=placed, out_specs=P("tm", None, "space", None), check_vma=False
    )
```
